512 devices in a mesh: dp: 32 (over x, z), sx: 8 (over y), sy: 2 (over core).
Axes of the slice: x: 4, y: 8, z: 8, core: 2. Of those that a mesh axis runs over, the one named last changes fastest.
Arguments:
- features: bfloat16 [32, 128, 16, 8, 128], P('dp', None, 'sx', 'sy'), may hold values from -6 to 6
- cotangent: bfloat16 [32, 128, 16, 8, 128], P('dp', None, 'sx', 'sy'), may hold values from -6 to 6
- weights: bfloat16 [27, 128, 128], replicated, may hold values from -0.109375 to 0.109375
- conv_bias: float32 [128], replicated, may hold values from -3 to 3
- error_state: float32 [32, 8, 2, 128, 3456], P('dp', 'sx', 'sy'), may hold values from -96 to 96
- warm_factor: float32 [4, 3456], replicated, may hold values from -6 to 6
Outputs:
- activation: bfloat16 [32, 128, 16, 8, 128], P('dp', None, 'sx', 'sy')
- input_grad: bfloat16 [32, 128, 16, 8, 128], P('dp', None, 'sx', 'sy')
- bias_grad: float32 [128], replicated
- factor_p: float32 [4, 128], replicated
- factor_q: float32 [4, 3456], replicated
- new_error: float32 [32, 8, 2, 128, 3456], P('dp', 'sx', 'sy')
The draws below stay inside these ranges and needn't reach their ends.
All inputs are finite; a program needn't handle non-finite values.
Results may differ from the reference program's by a relative error of at most 0.006.
Values may be sent and summed in bfloat16 or wider, within the bound.
No kernel may reach another device: no remote copies, remote signals or barrier semaphores. Data moves between devices by JAX's collectives and lax.ppermute only.
A program may use at most 64 MiB of HBM per device.

```python
import jax
import jax.numpy as jnp
from jax import lax

C = 128
TAPS = 27
RANK = 4
CX = 2
CY = 4
CZ = 128
NX = 16
NY = 8
N_DP = 32
N_SX = 8
N_SY = 2


def block_scale(rng, dims, pieces, least, high):
    def one(position, blocks):
        draws = jax.random.uniform(jax.random.fold_in(jax.random.fold_in(rng, 6), position), (blocks,), jnp.float32, least / len(pieces), high / len(pieces))
        return jnp.repeat(jnp.exp(draws), dims[position] // blocks).reshape((-1,) + (1,) * (len(dims) - position - 1))

    factor_of = one(*pieces[0])
    for cut in pieces[1:]:
        factor_of = factor_of * one(*cut)
    return factor_of


def bell_draw(key, dims, width, limit, cuts=(), held_as=jnp.bfloat16):
    values = width * jax.random.normal(key, dims, jnp.float32)
    if cuts:
        values = values * block_scale(key, dims, cuts, -0.22, 0.18)
    return jnp.clip(values, -limit, limit).astype(held_as)


def setup_inputs(seed: int = 0) -> dict:
    seeds = jax.random.split(jax.random.key(seed), 7)
    features = bell_draw(seeds[0], (N_DP, C, NX, NY, CZ), 1.0, 6.0, ((0, 32), (2, 8), (3, 2)))
    cotangent = bell_draw(seeds[1], (N_DP, C, NX, NY, CZ), 1.0, 6.0, ((0, 32), (2, 8), (3, 2)))
    weights = bell_draw(seeds[2], (TAPS, C, C), (TAPS * C) ** -0.5, 0.109375)
    conv_bias = bell_draw(seeds[3], (C,), 0.5, 3.0, (), jnp.float32)
    error_state = bell_draw(seeds[4], (N_DP, N_SX, N_SY, C, TAPS * C), 16.0, 96.0, ((0, 32), (1, 8), (2, 2)), jnp.float32)
    warm_factor = bell_draw(seeds[5], (RANK, TAPS * C), 1.0, 6.0, (), jnp.float32)
    return {"features": features, "cotangent": cotangent, "weights": weights, "conv_bias": conv_bias, "error_state": error_state, "warm_factor": warm_factor}


tap_offsets = tuple(((first, second, third) for first in range(3) for second in range(3) for third in range(3)))

def orthonormal(rows):
    result = []
    for column in range(rows.shape[0]):
        vector = rows[column]
        for basis in result:
            vector = vector - jnp.sum(basis * vector) * basis
        vector = vector / jnp.sqrt(jnp.sum(vector * vector) + 1e-06)
        result.append(vector)
    return jnp.stack(result)

def reference(features, cotangent, weights, conv_bias, error_state, warm_factor):
    pads = ((0, 0), (1, 1), (1, 1), (1, 1))

    def crop_pass(operands):
        inputs, upstream = operands
        padded = jnp.pad(inputs, pads)
        total = jnp.zeros((C, NX * NY * CZ), jnp.float32)
        for tap_index, (shift_x, shift_y, shift_z) in enumerate(tap_offsets):
            window = padded[:, shift_x:shift_x + NX, shift_y:shift_y + NY, shift_z:shift_z + CZ].reshape(C, -1)
            total = total + jnp.dot(weights[tap_index], window, preferred_element_type=jnp.float32)
        pre = total + conv_bias[:, None]
        activation = jax.nn.silu(pre).astype(jnp.bfloat16)
        sigma = jax.nn.sigmoid(pre)
        grad_pre = (upstream.reshape(C, -1).astype(jnp.float32) * sigma * (1.0 + pre * (1.0 - sigma))).astype(jnp.bfloat16)
        grad_padded = jnp.pad(grad_pre.reshape(C, NX, NY, CZ), pads)
        back = jnp.zeros((C, NX * NY * CZ), jnp.float32)
        for tap_index, (shift_x, shift_y, shift_z) in enumerate(tap_offsets):
            window = grad_padded[:, 2 - shift_x:2 - shift_x + NX, 2 - shift_y:2 - shift_y + NY, 2 - shift_z:2 - shift_z + CZ].reshape(C, -1)
            back = back + jnp.dot(weights[tap_index].T, window, preferred_element_type=jnp.float32)
        grad_blocks = grad_pre.astype(jnp.float32).reshape(C, N_SX, CX, N_SY, CY, CZ)
        partial_list = []
        for tap_index, (shift_x, shift_y, shift_z) in enumerate(tap_offsets):
            window = padded[:, shift_x:shift_x + NX, shift_y:shift_y + NY, shift_z:shift_z + CZ]
            window = window.astype(jnp.float32).reshape(C, N_SX, CX, N_SY, CY, CZ)
            partial_list.append(jnp.einsum('caxbyz,daxbyz->abdc', window, grad_blocks, precision=lax.Precision.HIGHEST))
        partials = jnp.stack(partial_list, axis=3).reshape(N_SX, N_SY, C, TAPS * C)
        bias_part = lax.optimization_barrier(jnp.sum(grad_pre.astype(jnp.float32), axis=1))
        return (activation.reshape(C, NX, NY, CZ), back.astype(jnp.bfloat16).reshape(C, NX, NY, CZ), partials, bias_part)
    activation, input_grad, partials, bias_parts = lax.map(crop_pass, (features, cotangent))
    devices_count = N_DP * N_SX * N_SY
    merged = partials + error_state
    psum = jnp.einsum('abcdk,rk->rd', merged, warm_factor, precision=lax.Precision.HIGHEST)
    factor_p = orthonormal(psum)
    q_terms = jnp.einsum('rd,abcdk->abcrk', factor_p, merged, precision=lax.Precision.HIGHEST)
    factor_q = lax.optimization_barrier(jnp.sum(q_terms, axis=(0, 1, 2))) / devices_count
    new_error = merged - jnp.einsum('rd,abcrk->abcdk', factor_p, q_terms, precision=lax.Precision.HIGHEST)
    bias_grad = lax.optimization_barrier(jnp.sum(bias_parts, axis=0)) / devices_count
    return (activation, input_grad, bias_grad, factor_p, factor_q, new_error)
```

```python
import jax
import jax.numpy as jnp
from jax import lax
from jax.experimental import pallas as pl
from jax.experimental.pallas import tpu as pltpu
from jax.sharding import Mesh
from jax.sharding import PartitionSpec as P

DP = ("dp_0", "dp_1")
ALL_AXES = ("dp_0", "dp_1", "sx", "sy")
C = 128
CX = 2
CY = 4
CZ = 128
PX = CX + 2
PY = CY + 2
TAPS = 27
K = TAPS * C
RANK = 4
GROUP = 3 * C
F32 = jnp.float32
BF16 = jnp.bfloat16
NT = (((1,), (1,)), ((), ()))
NN = (((1,), (0,)), ((), ()))
TN = (((0,), (0,)), ((), ()))
HIGHEST = lax.Precision.HIGHEST
VMEM = pl.BlockSpec(memory_space=pltpu.VMEM)
SMEM = pl.BlockSpec(memory_space=pltpu.SMEM)
PARAMS = pltpu.CompilerParams(vmem_limit_bytes=48 * 1024 * 1024)


def fill_planes(side, planes, own, low, high, across):
    lane = lax.broadcasted_iota(jnp.int32, (C, CZ), 1)
    zero = jnp.zeros((C, CZ), F32)

    def put(xp, yp, block):
        where = pl.ds((xp * PY + yp) * CZ, CZ)
        wide = block.astype(F32)
        before = jnp.where(lane == 0, zero, pltpu.roll(wide, 1, 1))
        after = jnp.where(lane == CZ - 1, zero, pltpu.roll(wide, CZ - 1, 1))
        planes[pl.ds(0, C), where] = before.astype(BF16)
        planes[pl.ds(C, C), where] = block
        planes[pl.ds(2 * C, C), where] = after.astype(BF16)

    first = side == 0
    for xp in range(PX):
        source = low if xp == 0 else high if xp == PX - 1 else own.at[xp - 1]
        for y in range(CY):
            put(xp, y + 1, source[y])
        edge = across[xp]
        nothing = jnp.zeros_like(edge)
        put(xp, 0, jnp.where(first, nothing, edge))
        put(xp, PY - 1, jnp.where(first, edge, nothing))


def window(planes, x, a, b):
    return planes[:, pl.ds(((x + a) * PY + b) * CZ, CY * CZ)]


def convolve(planes, lhs, x):
    total = None
    for a in range(3):
        for b in range(3):
            part = lax.dot_general(
                lhs[:, pl.ds((3 * a + b) * GROUP, GROUP)],
                window(planes, x, a, b),
                NN,
                preferred_element_type=F32,
            )
            total = part if total is None else total + part
    return total


def forward_kernel(
    side, own, low, high, across, upstream, lhs, bias, error, warm, act, grad, merged, sums, planes
):
    fill_planes(side[0], planes, own, low, high, across)
    grads = []
    bias_sum = jnp.zeros((C, CZ), F32)
    for x in range(CX):
        pre = convolve(planes, lhs, x) + bias[...]
        sigma = jax.nn.sigmoid(pre)
        active = (pre * sigma).astype(BF16)
        slope = sigma * (1.0 + pre * (1.0 - sigma))
        pieces = []
        for y in range(CY):
            span = slice(y * CZ, (y + 1) * CZ)
            act[x, y] = active[:, span]
            piece = (upstream[x, y].astype(F32) * slope[:, span]).astype(BF16)
            grad[x, y] = piece
            bias_sum = bias_sum + piece.astype(F32)
            pieces.append(piece)
        grads.append(jnp.concatenate(pieces, axis=1))
    for a in range(3):
        for b in range(3):
            span = pl.ds((3 * a + b) * GROUP, GROUP)
            part = error[:, span]
            for x in range(CX):
                part = part + lax.dot_general(
                    grads[x], window(planes, x, a, b), NT, preferred_element_type=F32
                )
            merged[:, span] = part
    local = lax.dot_general(
        warm[...], merged[...], NT, precision=HIGHEST, preferred_element_type=F32
    )
    sums[pl.ds(0, RANK), :] = local
    row = lax.dot_general(
        jnp.ones((8, CZ), F32), bias_sum, NT, precision=HIGHEST, preferred_element_type=F32
    )
    sums[pl.ds(RANK, RANK), :] = row[:RANK]


def project_kernel(sums, merged, factor_p, local_q, new_error):
    rows = []
    for r in range(RANK):
        vector = sums[pl.ds(r, 1), :]
        for basis in rows:
            vector = vector - jnp.sum(basis * vector) * basis
        vector = vector / jnp.sqrt(jnp.sum(vector * vector) + 1e-06)
        rows.append(vector)
        factor_p[pl.ds(r, 1), :] = vector
    basis = factor_p[...]
    q = lax.dot_general(basis, merged[...], NN, precision=HIGHEST, preferred_element_type=F32)
    local_q[...] = q
    new_error[...] = merged[...] - lax.dot_general(
        basis, q, TN, precision=HIGHEST, preferred_element_type=F32
    )


def backward_kernel(side, own, low, high, across, lhs, out, planes):
    fill_planes(side[0], planes, own, low, high, across)
    for x in range(CX):
        total = convolve(planes, lhs, x).astype(BF16)
        for y in range(CY):
            out[x, y] = total[:, y * CZ : (y + 1) * CZ]


def exchange(own, first):
    count = lax.axis_size("sx")
    up = [(i, i + 1) for i in range(count - 1)]
    down = [(i + 1, i) for i in range(count - 1)]
    low = lax.ppermute(own[CX - 1], "sx", up)
    high = lax.ppermute(own[0], "sx", down)
    slabs = jnp.concatenate([low[None], own, high[None]], axis=0)
    edge = jnp.where(first, slabs[:, CY - 1], slabs[:, 0])
    across = lax.ppermute(edge, "sy", [(0, 1), (1, 0)])
    return low, high, across


def reduce_all(x, axes):
    for axis in axes:
        x = lax.psum(x, axis)
    return x


def shards(features, cotangent, weights, conv_bias, error_state, warm_factor):
    side = lax.axis_index("sy").astype(jnp.int32)
    first = side == 0
    side = side.reshape(1)
    inputs = jnp.transpose(features[0], (1, 2, 0, 3))
    upstream = jnp.transpose(cotangent[0], (1, 2, 0, 3))
    lhs = jnp.transpose(weights, (1, 0, 2)).reshape(C, K)
    lhs_back = jnp.transpose(weights[::-1], (2, 0, 1)).reshape(C, K)
    low, high, across = exchange(inputs, first)
    block = jax.ShapeDtypeStruct((CX, CY, C, CZ), BF16)
    planes = pltpu.VMEM((GROUP, PX * PY * CZ), BF16)
    act, grad, merged, sums = pl.pallas_call(
        forward_kernel,
        out_shape=(
            block,
            block,
            jax.ShapeDtypeStruct((C, K), F32),
            jax.ShapeDtypeStruct((2 * RANK, C), F32),
        ),
        in_specs=[SMEM] + [VMEM] * 9,
        out_specs=(VMEM,) * 4,
        scratch_shapes=[planes],
        compiler_params=PARAMS,
        name="forward",
    )(
        side, inputs, low, high, across, upstream, lhs, conv_bias[:, None],
        error_state[0, 0, 0], warm_factor,
    )
    sums = reduce_all(sums, ("sy", "dp_0", "dp_1", "sx"))
    factor_p, local_q, new_error = pl.pallas_call(
        project_kernel,
        out_shape=(
            jax.ShapeDtypeStruct((RANK, C), F32),
            jax.ShapeDtypeStruct((RANK, K), F32),
            jax.ShapeDtypeStruct((C, K), F32),
        ),
        in_specs=[VMEM] * 2,
        out_specs=(VMEM,) * 3,
        compiler_params=PARAMS,
        name="project",
    )(sums, merged)
    g_low, g_high, g_across = exchange(grad, first)
    input_grad = pl.pallas_call(
        backward_kernel,
        out_shape=block,
        in_specs=[SMEM] + [VMEM] * 5,
        out_specs=VMEM,
        scratch_shapes=[planes],
        compiler_params=PARAMS,
        name="backward",
    )(side, grad, g_low, g_high, g_across, lhs_back)
    devices = 1
    for axis in ALL_AXES:
        devices = devices * lax.axis_size(axis)
    factor_q = reduce_all(local_q, ("sy", "dp_0", "dp_1", "sx")) / devices
    bias_grad = sums[RANK] / devices
    return (
        jnp.transpose(act, (2, 0, 1, 3))[None],
        jnp.transpose(input_grad, (2, 0, 1, 3))[None],
        bias_grad,
        factor_p,
        factor_q,
        new_error[None, None, None],
    )


def solution(mesh):
    torus = Mesh(mesh.devices.reshape(4, 8, mesh.shape["sx"], mesh.shape["sy"]), ALL_AXES)
    split = P(DP, None, "sx", "sy", None)
    state = P(DP, "sx", "sy", None, None)
    return jax.shard_map(
        shards,
        mesh=torus,
        in_specs=(split, split, P(), P(), state, P()),
        out_specs=(split, split, P(), P(), P(), state),
        check_vma=False,
    )
```

```python
import functools

import jax
import jax.numpy as jnp
from jax import lax
from jax.experimental import pallas as pl
from jax.experimental.pallas import tpu as pltpu
from jax.sharding import Mesh
from jax.sharding import PartitionSpec as P

DP = ("dp_0", "dp_1")
BLOCK = ("sx", "sy")
ALL_AXES = ("dp_0", "dp_1", "sx", "sy")
C = 128
CX = 2
CY = 4
CZ = 128
PX = CX + 2
PY = CY + 2
TAPS = 27
K = TAPS * C
RANK = 4
GROUP = 3 * C
F32 = jnp.float32
BF16 = jnp.bfloat16
NT = (((1,), (1,)), ((), ()))
NN = (((1,), (0,)), ((), ()))
TN = (((0,), (0,)), ((), ()))
HIGHEST = lax.Precision.HIGHEST
VMEM = pl.BlockSpec(memory_space=pltpu.VMEM)
SMEM = pl.BlockSpec(memory_space=pltpu.SMEM)
PARAMS = pltpu.CompilerParams(vmem_limit_bytes=48 * 1024 * 1024)


def fill_planes(side, planes, own, low, high, across):
    lane = lax.broadcasted_iota(jnp.int32, (C, CZ), 1)
    zero = jnp.zeros((C, CZ), F32)

    def put(xp, yp, block):
        where = pl.ds((xp * PY + yp) * CZ, CZ)
        wide = block.astype(F32)
        before = jnp.where(lane == 0, zero, pltpu.roll(wide, 1, 1))
        after = jnp.where(lane == CZ - 1, zero, pltpu.roll(wide, CZ - 1, 1))
        planes[pl.ds(0, C), where] = before.astype(BF16)
        planes[pl.ds(C, C), where] = block
        planes[pl.ds(2 * C, C), where] = after.astype(BF16)

    first = side == 0
    for xp in range(PX):
        source = low if xp == 0 else high if xp == PX - 1 else own.at[xp - 1]
        for y in range(CY):
            put(xp, y + 1, source[y])
        edge = across[xp]
        nothing = jnp.zeros_like(edge)
        put(xp, 0, jnp.where(first, nothing, edge))
        put(xp, PY - 1, jnp.where(first, edge, nothing))


def window(planes, x, a, b):
    return planes[:, pl.ds(((x + a) * PY + b) * CZ, CY * CZ)]


def convolve(planes, lhs, x):
    total = None
    for a in range(3):
        for b in range(3):
            part = lax.dot_general(
                lhs[:, pl.ds((3 * a + b) * GROUP, GROUP)],
                window(planes, x, a, b),
                NN,
                preferred_element_type=F32,
            )
            total = part if total is None else total + part
    return total


def forward_kernel(side, own, low, high, across, upstream, lhs, bias, act, grad, planes):
    fill_planes(side[0], planes, own, low, high, across)
    for x in range(CX):
        pre = convolve(planes, lhs, x) + bias[...]
        sigma = jax.nn.sigmoid(pre)
        active = (pre * sigma).astype(BF16)
        slope = sigma * (1.0 + pre * (1.0 - sigma))
        for y in range(CY):
            span = slice(y * CZ, (y + 1) * CZ)
            act[x, y] = active[:, span]
            grad[x, y] = (upstream[x, y].astype(F32) * slope[:, span]).astype(BF16)


def gradient_kernel(grad, planes, error, warm, merged, sums):
    grads = []
    bias_sum = jnp.zeros((C, CZ), F32)
    for x in range(CX):
        grads.append(jnp.concatenate([grad[x, y] for y in range(CY)], axis=1))
        for y in range(CY):
            bias_sum = bias_sum + grad[x, y].astype(F32)
    for a in range(3):
        for b in range(3):
            span = pl.ds((3 * a + b) * GROUP, GROUP)
            part = error[:, span]
            for x in range(CX):
                part = part + lax.dot_general(
                    grads[x], window(planes, x, a, b), NT, preferred_element_type=F32
                )
            merged[:, span] = part
    local = lax.dot_general(
        warm[...], merged[...], NT, precision=HIGHEST, preferred_element_type=F32
    )
    row = lax.dot_general(
        jnp.ones((8, CZ), F32), bias_sum, NT, precision=HIGHEST, preferred_element_type=F32
    )
    both = jnp.concatenate([local, row[:RANK]], axis=0)
    for copy in range(sums.shape[0]):
        sums[copy] = both


def fold_kernel(parts, copies):
    total = parts[0]
    for source in range(1, parts.shape[0]):
        total = total + parts[source]
    for copy in range(copies.shape[0]):
        copies[copy] = total


def project_kernel(parts, merged, factor_p, bias_grad, blocks, new_error, *, devices):
    sums = parts[0]
    for source in range(1, parts.shape[0]):
        sums = sums + parts[source]
    bias_grad[...] = sums[RANK : RANK + 1] / devices
    rows = []
    for r in range(RANK):
        vector = sums[r : r + 1]
        for basis in rows:
            vector = vector - jnp.sum(basis * vector) * basis
        vector = vector / jnp.sqrt(jnp.sum(vector * vector) + 1e-06)
        rows.append(vector)
        factor_p[pl.ds(r, 1), :] = vector
    basis = factor_p[...]
    q = lax.dot_general(basis, merged[...], NN, precision=HIGHEST, preferred_element_type=F32)
    for block in range(blocks.shape[0]):
        if block < TAPS:
            blocks[block] = q[:, block * C : (block + 1) * C]
        else:
            blocks[block] = jnp.zeros((RANK, C), F32)
    new_error[...] = merged[...] - lax.dot_general(
        basis, q, TN, precision=HIGHEST, preferred_element_type=F32
    )


def finish_kernel(blocks, factor_q, *, devices):
    for tap in range(TAPS):
        factor_q[:, pl.ds(tap * C, C)] = blocks[tap] / devices


def backward_kernel(side, own, low, high, across, lhs, out, planes):
    fill_planes(side[0], planes, own, low, high, across)
    for x in range(CX):
        total = convolve(planes, lhs, x).astype(BF16)
        for y in range(CY):
            out[x, y] = total[:, y * CZ : (y + 1) * CZ]


def exchange(own, first):
    count = lax.axis_size("sx")
    up = [(i, i + 1) for i in range(count - 1)]
    down = [(i + 1, i) for i in range(count - 1)]
    low = lax.ppermute(own[CX - 1], "sx", up)
    high = lax.ppermute(own[0], "sx", down)
    slabs = jnp.concatenate([low[None], own, high[None]], axis=0)
    edge = jnp.where(first, slabs[:, CY - 1], slabs[:, 0])
    across = lax.ppermute(edge, "sy", [(0, 1), (1, 0)])
    return low, high, across


def size_of(axes):
    count = 1
    for axis in axes:
        count = count * lax.axis_size(axis)
    return count


def swap(x, axes):
    return lax.all_to_all(x, axes, 0, 0, tiled=True)


def call(kernel, name, shapes, args, scalars=0, scratch=()):
    return pl.pallas_call(
        kernel,
        out_shape=shapes,
        in_specs=[SMEM] * scalars + [VMEM] * (len(args) - scalars),
        out_specs=jax.tree.map(lambda _: VMEM, shapes),
        scratch_shapes=list(scratch),
        compiler_params=PARAMS,
        name=name,
    )(*args)


def fold(parts, count):
    shape = jax.ShapeDtypeStruct((count,) + parts.shape[1:], F32)
    return call(fold_kernel, "fold", shape, (parts,))


def shards(features, cotangent, weights, conv_bias, error_state, warm_factor):
    side = lax.axis_index("sy").astype(jnp.int32)
    first = side == 0
    side = side.reshape(1)
    chips, columns = size_of(DP), size_of(BLOCK)
    devices = chips * columns
    inputs = jnp.transpose(features[0], (1, 2, 0, 3))
    upstream = jnp.transpose(cotangent[0], (1, 2, 0, 3))
    lhs = jnp.transpose(weights, (1, 0, 2)).reshape(C, K)
    lhs_back = jnp.transpose(weights[::-1], (2, 0, 1)).reshape(C, K)
    low, high, across = exchange(inputs, first)
    block = jax.ShapeDtypeStruct((CX, CY, C, CZ), BF16)
    plane_shape = (GROUP, PX * PY * CZ)
    act, grad, planes = call(
        forward_kernel,
        "forward",
        (block, block, jax.ShapeDtypeStruct(plane_shape, BF16)),
        (side, inputs, low, high, across, upstream, lhs, conv_bias[:, None]),
        scalars=1,
    )
    g_low, g_high, g_across = exchange(grad, first)
    merged, sums = call(
        gradient_kernel,
        "gradient",
        (
            jax.ShapeDtypeStruct((C, K), F32),
            jax.ShapeDtypeStruct((chips, 2 * RANK, C), F32),
        ),
        (grad, planes, error_state[0, 0, 0], warm_factor),
    )
    parts = swap(fold(swap(sums, DP), columns), BLOCK)
    padded = -(-TAPS // columns) * columns
    factor_p, bias_grad, blocks, new_error = call(
        functools.partial(project_kernel, devices=devices),
        "project",
        (
            jax.ShapeDtypeStruct((RANK, C), F32),
            jax.ShapeDtypeStruct((1, C), F32),
            jax.ShapeDtypeStruct((padded, RANK, C), F32),
            jax.ShapeDtypeStruct((C, K), F32),
        ),
        (parts, merged),
    )
    input_grad = call(
        backward_kernel,
        "backward",
        block,
        (side, grad, g_low, g_high, g_across, lhs_back),
        scalars=1,
        scratch=[pltpu.VMEM(plane_shape, BF16)],
    )
    width = padded // columns * RANK
    mine = fold(swap(blocks, BLOCK).reshape(columns, width, C), chips)
    mine = fold(swap(mine, DP), columns)
    blocks = swap(mine, BLOCK).reshape(padded, RANK, C)
    factor_q = call(
        functools.partial(finish_kernel, devices=devices),
        "finish",
        jax.ShapeDtypeStruct((RANK, K), F32),
        (blocks,),
    )
    return (
        jnp.transpose(act, (2, 0, 1, 3))[None],
        jnp.transpose(input_grad, (2, 0, 1, 3))[None],
        bias_grad[0],
        factor_p,
        factor_q,
        new_error[None, None, None],
    )


def solution(mesh):
    torus = Mesh(mesh.devices.reshape(4, 8, mesh.shape["sx"], mesh.shape["sy"]), ALL_AXES)
    split = P(DP, None, "sx", "sy", None)
    state = P(DP, "sx", "sy", None, None)
    return jax.shard_map(
        shards,
        mesh=torus,
        in_specs=(split, split, P(), P(), state, P()),
        out_specs=(split, split, P(), P(), P(), state),
        check_vma=False,
    )
```

```python
import functools

import jax
import jax.numpy as jnp
from jax import lax
from jax.experimental import pallas as pl
from jax.experimental.pallas import tpu as pltpu
from jax.sharding import Mesh
from jax.sharding import PartitionSpec as P

DP = ("dp_0", "dp_1")
BLOCK = ("sx", "sy")
ALL_AXES = ("dp_0", "dp_1", "sx", "sy")
C = 128
CX = 2
CY = 4
CZ = 128
PX = CX + 2
PY = CY + 2
TAPS = 27
K = TAPS * C
RANK = 4
GROUP = 3 * C
EXTRA = 4 * RANK
F32 = jnp.float32
BF16 = jnp.bfloat16
NT = (((1,), (1,)), ((), ()))
NN = (((1,), (0,)), ((), ()))
TN = (((0,), (0,)), ((), ()))
HIGHEST = lax.Precision.HIGHEST
VMEM = pl.BlockSpec(memory_space=pltpu.VMEM)
MIB = 1024 * 1024


def fill_planes(planes, low, own_0, own_1, high, across):
    lane = lax.broadcasted_iota(jnp.int32, (C, CZ), 1)
    zero = jnp.zeros((C, CZ), F32)

    def put(xp, yp, block):
        where = pl.ds((xp * PY + yp) * CZ, CZ)
        wide = block.astype(F32)
        before = jnp.where(lane == 0, zero, pltpu.roll(wide, 1, 1))
        after = jnp.where(lane == CZ - 1, zero, pltpu.roll(wide, CZ - 1, 1))
        planes[pl.ds(0, C), where] = before.astype(BF16)
        planes[pl.ds(C, C), where] = block
        planes[pl.ds(2 * C, C), where] = after.astype(BF16)

    first = lax.axis_index("sy") == 0
    for xp, source in enumerate((low, own_0, own_1, high)):
        for y in range(CY):
            put(xp, y + 1, source[y])
        edge = across[xp]
        nothing = jnp.zeros_like(edge)
        put(xp, 0, jnp.where(first, nothing, edge))
        put(xp, PY - 1, jnp.where(first, edge, nothing))


def window(planes, x, a, b):
    return planes[:, pl.ds(((x + a) * PY + b) * CZ, CY * CZ)]


def convolve(planes, lhs, x):
    total = None
    for a in range(3):
        for b in range(3):
            part = lax.dot_general(
                lhs[:, pl.ds((3 * a + b) * GROUP, GROUP)],
                window(planes, x, a, b),
                NN,
                preferred_element_type=F32,
            )
            total = part if total is None else total + part
    return total


def pieces(x):
    first = x.astype(BF16).astype(F32)
    rest = x - first
    second = rest.astype(BF16).astype(F32)
    third = (rest - second).astype(BF16).astype(F32)
    return first, second, third


def prepare_kernel(weights, warm, error, bias, lhs, base, bias_plane):
    bias_plane[...] = jnp.transpose(jnp.broadcast_to(bias[...], (C, C)))
    for tap in range(TAPS):
        lhs[pl.ds(0, C), pl.ds(tap * C, C)] = weights[tap]
    rows = warm[...]
    first, second, third = pieces(rows)
    stacked = jnp.concatenate([first, second, third, jnp.zeros_like(rows)], axis=0)
    lhs[pl.ds(C, EXTRA), :] = stacked.astype(BF16)
    base[...] = lax.dot_general(rows, error[...], NT, precision=HIGHEST, preferred_element_type=F32)


def forward_kernel(
    low, own_0, own_1, high, across, upstream, lhs, bias, base,
    act, grad_0, grad_1, sums, planes,
):
    fill_planes(planes, low, own_0, own_1, high, across)
    joint = jnp.zeros((EXTRA, C), F32)
    for x, grad in enumerate((grad_0, grad_1)):
        total = convolve(planes, lhs, x)
        pre = total[:C] + bias[:, :1]
        sigma = jax.nn.sigmoid(pre)
        active = (pre * sigma).astype(BF16)
        slope = sigma * (1.0 + pre * (1.0 - sigma))
        grads = []
        for y in range(CY):
            span = slice(y * CZ, (y + 1) * CZ)
            act[x, y] = active[:, span]
            piece = (upstream[x, y].astype(F32) * slope[:, span]).astype(BF16)
            grad[y] = piece
            grads.append(piece)
        field = total[C : C + RANK] + total[C + RANK : C + 2 * RANK]
        field = field + total[C + 2 * RANK : C + 3 * RANK]
        first, second, third = pieces(field)
        stacked = jnp.concatenate([first, second, third, jnp.ones_like(field)], axis=0)
        joint = joint + lax.dot_general(
            stacked.astype(BF16), jnp.concatenate(grads, axis=1), NT, preferred_element_type=F32
        )
    local = joint[:RANK] + joint[RANK : 2 * RANK] + joint[2 * RANK : 3 * RANK] + base[...]
    both = jnp.concatenate([local, joint[3 * RANK :]], axis=0)
    for copy in range(sums.shape[0]):
        sums[copy] = both


def gradient_kernel(
    low, own_0, own_1, high, across, grad_0, grad_1, error, merged, upper, lower, planes
):
    fill_planes(planes, low, own_0, own_1, high, across)
    grads = []
    for grad in (grad_0, grad_1):
        grads.append(jnp.concatenate([grad[y] for y in range(CY)], axis=1))
    for a in range(3):
        for b in range(3):
            span = pl.ds((3 * a + b) * GROUP, GROUP)
            part = error[:, span]
            for x in range(CX):
                part = part + lax.dot_general(
                    grads[x], window(planes, x, a, b), NT, preferred_element_type=F32
                )
            merged[:, span] = part
            rounded = part.astype(BF16)
            upper[:, span] = rounded
            lower[:, span] = (part - rounded.astype(F32)).astype(BF16)


def fold_kernel(parts, copies):
    total = parts[0]
    for source in range(1, parts.shape[0]):
        total = total + parts[source]
    for copy in range(copies.shape[0]):
        copies[copy] = total


def project_kernel(parts, upper, lower, factor_p, bias_grad, blocks, *, devices):
    sums = parts[0]
    for source in range(1, parts.shape[0]):
        sums = sums + parts[source]
    bias_grad[...] = sums[RANK : RANK + 1] / devices
    rows = []
    for r in range(RANK):
        vector = sums[r : r + 1]
        for basis in rows:
            vector = vector - jnp.sum(basis * vector) * basis
        vector = vector / jnp.sqrt(jnp.sum(vector * vector) + 1e-06)
        rows.append(vector)
        factor_p[pl.ds(r, 1), :] = vector
    basis = jnp.concatenate(rows, axis=0)
    first, second, third = pieces(basis)
    stacked = jnp.concatenate([first, second, third, jnp.zeros_like(basis)], axis=0).astype(BF16)
    q = lax.dot_general(stacked, upper[...], NN, preferred_element_type=F32)
    q = q + lax.dot_general(stacked, lower[...], NN, preferred_element_type=F32)
    q = q[:RANK] + q[RANK : 2 * RANK] + q[2 * RANK : 3 * RANK]
    for block in range(blocks.shape[0]):
        if block < TAPS:
            blocks[block] = q[:, block * C : (block + 1) * C]
        else:
            blocks[block] = jnp.zeros((RANK, C), F32)


def residual_kernel(basis, blocks, merged, new_error):
    for tap in range(TAPS):
        span = pl.ds(tap * C, C)
        new_error[:, span] = merged[:, span] - lax.dot_general(
            basis[...], blocks[tap], TN, precision=HIGHEST, preferred_element_type=F32
        )


def finish_kernel(blocks, factor_q, *, devices):
    for tap in range(TAPS):
        factor_q[:, pl.ds(tap * C, C)] = blocks[tap] / devices


def backward_kernel(low, own_0, own_1, high, across, weights, out, planes):
    fill_planes(planes, low, own_0, own_1, high, across)
    totals = [None] * CX
    for pair in range(9):
        taps = [TAPS - 1 - 3 * pair - c for c in range(3)]
        stack = jnp.concatenate([weights[tap] for tap in taps], axis=0)
        for x in range(CX):
            part = lax.dot_general(
                stack, window(planes, x, pair // 3, pair % 3), TN, preferred_element_type=F32
            )
            totals[x] = part if totals[x] is None else totals[x] + part
    for x in range(CX):
        total = totals[x].astype(BF16)
        for y in range(CY):
            out[x, y] = total[:, y * CZ : (y + 1) * CZ]


def edge_kernel(low, own_0, own_1, high, edge):
    first = lax.axis_index("sy") == 0
    for xp, source in enumerate((low, own_0, own_1, high)):
        edge[xp] = jnp.where(first, source[CY - 1], source[0])


def exchange_x(own_0, own_1):
    count = lax.axis_size("sx")
    up = [(i, i + 1) for i in range(count - 1)]
    down = [(i + 1, i) for i in range(count - 1)]
    return lax.ppermute(own_1, "sx", up), lax.ppermute(own_0, "sx", down)


def exchange_y(low, own_0, own_1, high):
    slab = jax.ShapeDtypeStruct((PX, C, CZ), BF16)
    edge = call(edge_kernel, "edge", 2, slab, (low, own_0, own_1, high))
    return lax.ppermute(edge, "sy", [(0, 1), (1, 0)])


tie = lax.optimization_barrier


def size_of(axes):
    count = 1
    for axis in axes:
        count = count * lax.axis_size(axis)
    return count


def swap(x, axes):
    return lax.all_to_all(x, axes, 0, 0, tiled=True)


def call(kernel, name, room, shapes, args, scratch=()):
    return pl.pallas_call(
        kernel,
        out_shape=shapes,
        in_specs=[VMEM] * len(args),
        out_specs=jax.tree.map(lambda _: VMEM, shapes),
        scratch_shapes=list(scratch),
        compiler_params=pltpu.CompilerParams(vmem_limit_bytes=room * MIB),
        name=name,
    )(*args)


def fold(parts, count):
    shape = jax.ShapeDtypeStruct((count,) + parts.shape[1:], F32)
    return call(fold_kernel, "fold", 2, shape, (parts,))


def f32(*shape):
    return jax.ShapeDtypeStruct(shape, F32)


def bf16(*shape):
    return jax.ShapeDtypeStruct(shape, BF16)


def shards(features, cotangent, weights, conv_bias, error_state, warm_factor):
    chips, columns = size_of(DP), size_of(BLOCK)
    devices = chips * columns
    padded = -(-TAPS // columns) * columns
    planes = pltpu.VMEM((GROUP, PX * PY * CZ), BF16)
    error = error_state[0, 0, 0]
    own_0 = jnp.transpose(features[0, :, 0], (1, 0, 2))
    own_1 = jnp.transpose(features[0, :, 1], (1, 0, 2))
    low, high = exchange_x(own_0, own_1)
    upstream = jnp.transpose(cotangent[0], (1, 2, 0, 3))
    lhs, base, bias = call(
        prepare_kernel,
        "prepare",
        8,
        (bf16(C + EXTRA, K), f32(RANK, C), f32(C, C)),
        (weights, warm_factor, error, conv_bias[None]),
    )
    low, high, lhs, base, bias, upstream = tie((low, high, lhs, base, bias, upstream))
    across = exchange_y(low, own_0, own_1, high)
    block = (low, own_0, own_1, high, across)
    act, grad_0, grad_1, sums = call(
        forward_kernel,
        "forward",
        10,
        (bf16(CX, CY, C, CZ), bf16(CY, C, CZ), bf16(CY, C, CZ), f32(chips, 2 * RANK, C)),
        (*block, upstream, lhs, bias, base),
        [planes],
    )
    parts = swap(sums, DP)
    g_low, g_high = exchange_x(grad_0, grad_1)
    merged, upper, lower = call(
        gradient_kernel,
        "gradient",
        14,
        (f32(C, K), bf16(C, K), bf16(C, K)),
        (*block, grad_0, grad_1, error),
        [planes],
    )
    parts, g_low, g_high, upper = tie((parts, g_low, g_high, upper))
    parts = swap(fold(parts, columns), BLOCK)
    g_across = exchange_y(g_low, grad_0, grad_1, g_high)
    input_grad = call(
        backward_kernel,
        "backward",
        8,
        bf16(CX, CY, C, CZ),
        (g_low, grad_0, grad_1, g_high, g_across, weights),
        [planes],
    )
    activation = jnp.transpose(act, (2, 0, 1, 3))[None]
    input_grad = jnp.transpose(input_grad, (2, 0, 1, 3))[None]
    parts, input_grad, activation = tie((parts, input_grad, activation))
    factor_p, bias_grad, blocks = call(
        functools.partial(project_kernel, devices=devices),
        "project",
        6,
        (f32(RANK, C), f32(1, C), f32(padded, RANK, C)),
        (parts, upper, lower),
    )
    new_error = call(
        residual_kernel, "residual", 6, f32(C, K), (factor_p, blocks, merged)
    )
    width = padded // columns * RANK
    mine, new_error = tie((swap(blocks, BLOCK), new_error))
    mine = fold(mine.reshape(columns, width, C), chips)
    mine = fold(swap(mine, DP), columns)
    blocks = swap(mine, BLOCK).reshape(padded, RANK, C)
    factor_q = call(
        functools.partial(finish_kernel, devices=devices), "finish", 2, f32(RANK, K), (blocks,)
    )
    return (
        activation,
        input_grad,
        bias_grad[0],
        factor_p,
        factor_q,
        new_error[None, None, None],
    )


def solution(mesh):
    torus = Mesh(mesh.devices.reshape(4, 8, mesh.shape["sx"], mesh.shape["sy"]), ALL_AXES)
    split = P(DP, None, "sx", "sy", None)
    state = P(DP, "sx", "sy", None, None)
    return jax.shard_map(
        shards,
        mesh=torus,
        in_specs=(split, split, P(), P(), state, P()),
        out_specs=(split, split, P(), P(), P(), state),
        check_vma=False,
    )
```

```python
import functools

import jax
import jax.numpy as jnp
from jax import lax
from jax.experimental import pallas as pl
from jax.experimental.pallas import tpu as pltpu
from jax.sharding import Mesh
from jax.sharding import PartitionSpec as P

DP = ("dp_0", "dp_1")
BLOCK = ("sx", "sy")
ALL_AXES = ("dp_0", "dp_1", "sx", "sy")
C = 128
CX = 2
CY = 4
CZ = 128
PX = CX + 2
PY = CY + 2
TAPS = 27
K = TAPS * C
RANK = 4
GROUP = 3 * C
EXTRA = 4 * RANK
F32 = jnp.float32
BF16 = jnp.bfloat16
NT = (((1,), (1,)), ((), ()))
NN = (((1,), (0,)), ((), ()))
TN = (((0,), (0,)), ((), ()))
HIGHEST = lax.Precision.HIGHEST
VMEM = pl.BlockSpec(memory_space=pltpu.VMEM)
HBM = pl.BlockSpec(memory_space=pltpu.HBM)
MIB = 1024 * 1024


def fill_planes(planes, low, own_0, own_1, high, across):
    lane = lax.broadcasted_iota(jnp.int32, (C, CZ), 1)
    zero = jnp.zeros((C, CZ), F32)

    def put(xp, yp, block):
        where = pl.ds((xp * PY + yp) * CZ, CZ)
        wide = block.astype(F32)
        before = jnp.where(lane == 0, zero, pltpu.roll(wide, 1, 1))
        after = jnp.where(lane == CZ - 1, zero, pltpu.roll(wide, CZ - 1, 1))
        planes[pl.ds(0, C), where] = before.astype(BF16)
        planes[pl.ds(C, C), where] = block
        planes[pl.ds(2 * C, C), where] = after.astype(BF16)

    first = lax.axis_index("sy") == 0
    for xp, source in enumerate((low, own_0, own_1, high)):
        for y in range(CY):
            put(xp, y + 1, source[y])
        edge = across[xp]
        nothing = jnp.zeros_like(edge)
        put(xp, 0, jnp.where(first, nothing, edge))
        put(xp, PY - 1, jnp.where(first, edge, nothing))


def window(planes, x, a, b):
    return planes[:, pl.ds(((x + a) * PY + b) * CZ, CY * CZ)]


def convolve(planes, lhs, x):
    total = None
    for a in range(3):
        for b in range(3):
            part = lax.dot_general(
                lhs[:, pl.ds((3 * a + b) * GROUP, GROUP)],
                window(planes, x, a, b),
                NN,
                preferred_element_type=F32,
            )
            total = part if total is None else total + part
    return total


def pieces(x):
    first = x.astype(BF16).astype(F32)
    rest = x - first
    second = rest.astype(BF16).astype(F32)
    third = (rest - second).astype(BF16).astype(F32)
    return first, second, third


def prepare_kernel(weights, warm, error, bias, lhs, base, bias_plane):
    bias_plane[...] = jnp.transpose(jnp.broadcast_to(bias[...], (C, C)))
    for tap in range(TAPS):
        lhs[pl.ds(0, C), pl.ds(tap * C, C)] = weights[tap]
    rows = warm[...]
    first, second, third = pieces(rows)
    stacked = jnp.concatenate([first, second, third, jnp.zeros_like(rows)], axis=0)
    lhs[pl.ds(C, EXTRA), :] = stacked.astype(BF16)
    base[...] = lax.dot_general(rows, error[...], NT, precision=HIGHEST, preferred_element_type=F32)


def forward_kernel(
    low, own_0, own_1, high, across, upstream, lhs, bias, base,
    act, grad_0, grad_1, sums, planes,
):
    fill_planes(planes, low, own_0, own_1, high, across)
    joint = jnp.zeros((EXTRA, C), F32)
    for x, grad in enumerate((grad_0, grad_1)):
        total = convolve(planes, lhs, x)
        pre = total[:C] + bias[:, :1]
        sigma = jax.nn.sigmoid(pre)
        active = (pre * sigma).astype(BF16)
        slope = sigma * (1.0 + pre * (1.0 - sigma))
        grads = []
        for y in range(CY):
            span = slice(y * CZ, (y + 1) * CZ)
            act[x, y] = active[:, span]
            piece = (upstream[x, y].astype(F32) * slope[:, span]).astype(BF16)
            grad[y] = piece
            grads.append(piece)
        field = total[C : C + RANK] + total[C + RANK : C + 2 * RANK]
        field = field + total[C + 2 * RANK : C + 3 * RANK]
        first, second, third = pieces(field)
        stacked = jnp.concatenate([first, second, third, jnp.ones_like(field)], axis=0)
        joint = joint + lax.dot_general(
            stacked.astype(BF16), jnp.concatenate(grads, axis=1), NT, preferred_element_type=F32
        )
    local = joint[:RANK] + joint[RANK : 2 * RANK] + joint[2 * RANK : 3 * RANK] + base[...]
    both = jnp.concatenate([local, joint[3 * RANK :]], axis=0)
    for copy in range(sums.shape[0]):
        sums[copy] = both


def gradient_kernel(wait, block, upper_out, lower_out, planes, upper, lower, sem):
    low, own_0, own_1, high, across, grad_0, grad_1, error = block
    wait(0, 1, 2, 3, 4)
    fill_planes(planes, low, own_0, own_1, high, across)
    wait(5, 6)
    grads = []
    for grad in (grad_0, grad_1):
        grads.append(jnp.concatenate([grad[y] for y in range(CY)], axis=1))
    wait(7)
    leaving = []
    for pair in range(9):
        span = pl.ds(pair * GROUP, GROUP)
        part = error[:, span]
        for x in range(CX):
            part = part + lax.dot_general(
                grads[x], window(planes, x, pair // 3, pair % 3), NT, preferred_element_type=F32
            )
        rounded = part.astype(BF16)
        upper[:, span] = rounded
        lower[:, span] = (part - rounded.astype(F32)).astype(BF16)
        for side, (held, out) in enumerate(((upper, upper_out), (lower, lower_out))):
            leaving.append(
                pltpu.make_async_copy(held.at[:, span], out.at[:, span], sem.at[2 * pair + side])
            )
            leaving[-1].start()
    for transfer in leaving:
        transfer.wait()


def fold_kernel(parts, copies):
    total = parts[0]
    for source in range(1, parts.shape[0]):
        total = total + parts[source]
    for copy in range(copies.shape[0]):
        copies[copy] = total


def project_kernel(wait, held, parts, factor_p, bias_grad, blocks, *, devices):
    upper, lower = held
    sums = parts[0]
    for source in range(1, parts.shape[0]):
        sums = sums + parts[source]
    bias_grad[...] = sums[RANK : RANK + 1] / devices
    rows = []
    for r in range(RANK):
        vector = sums[r : r + 1]
        for basis in rows:
            vector = vector - jnp.sum(basis * vector) * basis
        vector = vector / jnp.sqrt(jnp.sum(vector * vector) + 1e-06)
        rows.append(vector)
        factor_p[pl.ds(r, 1), :] = vector
    basis = jnp.concatenate(rows, axis=0)
    first, second, third = pieces(basis)
    stacked = jnp.concatenate([first, second, third, jnp.zeros_like(basis)], axis=0).astype(BF16)
    wait(0, 1)
    q = lax.dot_general(stacked, upper[...], NN, preferred_element_type=F32)
    q = q + lax.dot_general(stacked, lower[...], NN, preferred_element_type=F32)
    q = q[:RANK] + q[RANK : 2 * RANK] + q[2 * RANK : 3 * RANK]
    for block in range(blocks.shape[0]):
        if block < TAPS:
            blocks[block] = q[:, block * C : (block + 1) * C]
        else:
            blocks[block] = jnp.zeros((RANK, C), F32)


def residual_kernel(wait, held, out, new_error, sem):
    basis, blocks, upper, lower = held
    wait(0, 1, 2, 3)
    leaving = []
    for pair in range(9):
        span = pl.ds(pair * GROUP, GROUP)
        rows = jnp.concatenate([blocks[3 * pair + c] for c in range(3)], axis=1)
        merged = upper[:, span].astype(F32) + lower[:, span].astype(F32)
        new_error[:, span] = merged - lax.dot_general(
            basis[...], rows, TN, precision=HIGHEST, preferred_element_type=F32
        )
        leaving.append(pltpu.make_async_copy(new_error.at[:, span], out.at[:, span], sem.at[pair]))
        leaving[-1].start()
    for transfer in leaving:
        transfer.wait()


def finish_kernel(blocks, factor_q, *, devices):
    for tap in range(TAPS):
        factor_q[:, pl.ds(tap * C, C)] = blocks[tap] / devices


def backward_kernel(wait, held, out, planes):
    low, own_0, own_1, high, across, weights = held
    wait(0, 1, 2, 3, 4)
    fill_planes(planes, low, own_0, own_1, high, across)
    wait(5)
    totals = [None] * CX
    for pair in range(9):
        taps = [TAPS - 1 - 3 * pair - c for c in range(3)]
        stack = jnp.concatenate([weights[tap] for tap in taps], axis=0)
        for x in range(CX):
            part = lax.dot_general(
                stack, window(planes, x, pair // 3, pair % 3), TN, preferred_element_type=F32
            )
            totals[x] = part if totals[x] is None else totals[x] + part
    for x in range(CX):
        total = totals[x].astype(BF16)
        for y in range(CY):
            out[x, y] = total[:, y * CZ : (y + 1) * CZ]


def edge_kernel(low, own_0, own_1, high, edge):
    first = lax.axis_index("sy") == 0
    for xp, source in enumerate((low, own_0, own_1, high)):
        edge[xp] = jnp.where(first, source[CY - 1], source[0])


def exchange_x(own_0, own_1):
    count = lax.axis_size("sx")
    up = [(i, i + 1) for i in range(count - 1)]
    down = [(i + 1, i) for i in range(count - 1)]
    return lax.ppermute(own_1, "sx", up), lax.ppermute(own_0, "sx", down)


def exchange_y(low, own_0, own_1, high):
    slab = jax.ShapeDtypeStruct((PX, C, CZ), BF16)
    edge = call(edge_kernel, "edge", 2, slab, (low, own_0, own_1, high))
    return lax.ppermute(edge, "sy", [(0, 1), (1, 0)])


tie = lax.optimization_barrier


def size_of(axes):
    count = 1
    for axis in axes:
        count = count * lax.axis_size(axis)
    return count


def swap(x, axes):
    return lax.all_to_all(x, axes, 0, 0, tiled=True)


def call(kernel, name, room, shapes, args, scratch=(), outs=VMEM):
    return pl.pallas_call(
        kernel,
        out_shape=shapes,
        in_specs=[VMEM] * len(args),
        out_specs=jax.tree.map(lambda _: outs, shapes),
        scratch_shapes=list(scratch),
        compiler_params=pltpu.CompilerParams(vmem_limit_bytes=room * MIB),
        name=name,
    )(*args)


def fetch_and_call(kernel, name, room, shapes, args, scratch=(), outs=VMEM, near=()):
    count = len(args)

    def body(*refs):
        close, refs = refs[: len(near)], refs[len(near) :]
        sources, rest = refs[:count], refs[count:]
        results = len(jax.tree.leaves(shapes))
        held, sem = rest[results : results + count], rest[results + count]
        copies = [
            pltpu.make_async_copy(source, target, sem.at[k])
            for k, (source, target) in enumerate(zip(sources, held))
        ]
        for copy in copies:
            copy.start()

        def wait(*which):
            for k in which:
                copies[k].wait()

        kernel(wait, held, *close, *rest[:results], *rest[results + count + 1 :])

    return pl.pallas_call(
        body,
        out_shape=shapes,
        in_specs=[VMEM] * len(near) + [HBM] * count,
        out_specs=jax.tree.map(lambda _: outs, shapes),
        scratch_shapes=[
            *(pltpu.VMEM(arg.shape, arg.dtype) for arg in args),
            pltpu.SemaphoreType.DMA((count,)),
            *scratch,
        ],
        compiler_params=pltpu.CompilerParams(vmem_limit_bytes=room * MIB),
        name=name,
    )(*near, *args)


def fold(parts, count):
    shape = jax.ShapeDtypeStruct((count,) + parts.shape[1:], F32)
    return call(fold_kernel, "fold", 2, shape, (parts,))


def f32(*shape):
    return jax.ShapeDtypeStruct(shape, F32)


def bf16(*shape):
    return jax.ShapeDtypeStruct(shape, BF16)


def shards(features, cotangent, weights, conv_bias, error_state, warm_factor):
    chips, columns = size_of(DP), size_of(BLOCK)
    devices = chips * columns
    padded = -(-TAPS // columns) * columns
    planes = pltpu.VMEM((GROUP, PX * PY * CZ), BF16)
    error = error_state[0, 0, 0]
    own_0 = jnp.transpose(features[0, :, 0], (1, 0, 2))
    own_1 = jnp.transpose(features[0, :, 1], (1, 0, 2))
    low, high = exchange_x(own_0, own_1)
    upstream = jnp.transpose(cotangent[0], (1, 2, 0, 3))
    lhs, base, bias = call(
        prepare_kernel,
        "prepare",
        8,
        (bf16(C + EXTRA, K), f32(RANK, C), f32(C, C)),
        (weights, warm_factor, error, conv_bias[None]),
    )
    low, high, lhs, base, bias, upstream = tie((low, high, lhs, base, bias, upstream))
    across = exchange_y(low, own_0, own_1, high)
    block = (low, own_0, own_1, high, across)
    act, grad_0, grad_1, sums = call(
        forward_kernel,
        "forward",
        10,
        (bf16(CX, CY, C, CZ), bf16(CY, C, CZ), bf16(CY, C, CZ), f32(chips, 2 * RANK, C)),
        (*block, upstream, lhs, bias, base),
        [planes],
    )
    parts = swap(sums, DP)
    upper, lower = fetch_and_call(
        gradient_kernel,
        "gradient",
        60,
        (bf16(C, K), bf16(C, K)),
        (*block, grad_0, grad_1, error),
        [planes, pltpu.VMEM((C, K), BF16), pltpu.VMEM((C, K), BF16), pltpu.SemaphoreType.DMA((18,))],
        HBM,
    )
    parts, upper, lower, near_0, near_1 = tie((parts, upper, lower, grad_0, grad_1))
    parts = swap(fold(parts, columns), BLOCK)
    g_low, g_high = exchange_x(near_0, near_1)
    factor_p, bias_grad, blocks = fetch_and_call(
        functools.partial(project_kernel, devices=devices),
        "project",
        60,
        (f32(RANK, C), f32(1, C), f32(padded, RANK, C)),
        (upper, lower),
        near=(parts,),
    )
    new_error = fetch_and_call(
        residual_kernel,
        "residual",
        60,
        f32(C, K),
        (factor_p, blocks, upper, lower),
        [pltpu.VMEM((C, K), F32), pltpu.SemaphoreType.DMA((9,))],
        HBM,
    )
    width = padded // columns * RANK
    mine = swap(blocks, BLOCK)
    mine, new_error, g_low, g_high = tie((mine, new_error, g_low, g_high))
    mine = swap(fold(mine.reshape(columns, width, C), chips), DP)
    g_across = exchange_y(g_low, near_0, near_1, g_high)
    mine, g_across, act = tie((mine, g_across, act))
    blocks = swap(fold(mine, columns), BLOCK).reshape(padded, RANK, C)
    input_grad = fetch_and_call(
        backward_kernel,
        "backward",
        60,
        bf16(CX, CY, C, CZ),
        (g_low, near_0, near_1, g_high, g_across, weights),
        [planes],
    )
    activation = jnp.transpose(act, (2, 0, 1, 3))[None]
    input_grad = jnp.transpose(input_grad, (2, 0, 1, 3))[None]
    factor_q = call(
        functools.partial(finish_kernel, devices=devices), "finish", 2, f32(RANK, K), (blocks,)
    )
    return (
        activation,
        input_grad,
        bias_grad[0],
        factor_p,
        factor_q,
        new_error[None, None, None],
    )


def solution(mesh):
    torus = Mesh(mesh.devices.reshape(4, 8, mesh.shape["sx"], mesh.shape["sy"]), ALL_AXES)
    split = P(DP, None, "sx", "sy", None)
    state = P(DP, "sx", "sy", None, None)
    return jax.shard_map(
        shards,
        mesh=torus,
        in_specs=(split, split, P(), P(), state, P()),
        out_specs=(split, split, P(), P(), P(), state),
        check_vma=False,
    )
```

```python
import functools

import jax
import jax.numpy as jnp
from jax import lax
from jax.experimental import pallas as pl
from jax.experimental.pallas import tpu as pltpu
from jax.sharding import Mesh
from jax.sharding import PartitionSpec as P

DP = ("dp_0", "dp_1")
BLOCK = ("sx", "sy")
ALL_AXES = ("dp_0", "dp_1", "sx", "sy")
C = 128
CX = 2
CY = 4
CZ = 128
PX = CX + 2
PY = CY + 2
TAPS = 27
K = TAPS * C
RANK = 4
GROUP = 3 * C
EXTRA = 4 * RANK
F32 = jnp.float32
BF16 = jnp.bfloat16
NT = (((1,), (1,)), ((), ()))
NN = (((1,), (0,)), ((), ()))
TN = (((0,), (0,)), ((), ()))
HIGHEST = lax.Precision.HIGHEST
VMEM = pl.BlockSpec(memory_space=pltpu.VMEM)
HBM = pl.BlockSpec(memory_space=pltpu.HBM)
MIB = 1024 * 1024


def fill_planes(planes, low, own_0, own_1, high, across):
    lane = lax.broadcasted_iota(jnp.int32, (C, CZ), 1)
    zero = jnp.zeros((C, CZ), F32)

    def put(xp, yp, block):
        where = pl.ds((xp * PY + yp) * CZ, CZ)
        wide = block.astype(F32)
        before = jnp.where(lane == 0, zero, pltpu.roll(wide, 1, 1))
        after = jnp.where(lane == CZ - 1, zero, pltpu.roll(wide, CZ - 1, 1))
        planes[pl.ds(0, C), where] = before.astype(BF16)
        planes[pl.ds(C, C), where] = block
        planes[pl.ds(2 * C, C), where] = after.astype(BF16)

    first = lax.axis_index("sy") == 0
    for xp, source in enumerate((low, own_0, own_1, high)):
        for y in range(CY):
            put(xp, y + 1, source[y])
        edge = across[xp]
        nothing = jnp.zeros_like(edge)
        put(xp, 0, jnp.where(first, nothing, edge))
        put(xp, PY - 1, jnp.where(first, edge, nothing))


def window(planes, x, a, b):
    return planes[:, pl.ds(((x + a) * PY + b) * CZ, CY * CZ)]


def convolve(planes, lhs, x):
    total = None
    for a in range(3):
        for b in range(3):
            part = lax.dot_general(
                lhs[:, pl.ds((3 * a + b) * GROUP, GROUP)],
                window(planes, x, a, b),
                NN,
                preferred_element_type=F32,
            )
            total = part if total is None else total + part
    return total


def pieces(x):
    first = x.astype(BF16).astype(F32)
    rest = x - first
    second = rest.astype(BF16).astype(F32)
    third = (rest - second).astype(BF16).astype(F32)
    return first, second, third


def prepare_kernel(weights, warm, error, bias, lhs, base, bias_plane):
    bias_plane[...] = jnp.transpose(jnp.broadcast_to(bias[...], (C, C)))
    for tap in range(TAPS):
        lhs[pl.ds(0, C), pl.ds(tap * C, C)] = weights[tap]
    rows = warm[...]
    first, second, third = pieces(rows)
    stacked = jnp.concatenate([first, second, third, jnp.zeros_like(rows)], axis=0)
    lhs[pl.ds(C, EXTRA), :] = stacked.astype(BF16)
    base[...] = lax.dot_general(rows, error[...], NT, precision=HIGHEST, preferred_element_type=F32)


def forward_kernel(
    low, own_0, own_1, high, across, upstream, lhs, bias, base,
    act, grad_0, grad_1, edges, sums, planes,
):
    fill_planes(planes, low, own_0, own_1, high, across)
    first_core = lax.axis_index("sy") == 0
    joint = jnp.zeros((EXTRA, C), F32)
    for x, grad in enumerate((grad_0, grad_1)):
        total = convolve(planes, lhs, x)
        pre = total[:C] + bias[:, :1]
        sigma = jax.nn.sigmoid(pre)
        active = (pre * sigma).astype(BF16)
        slope = sigma * (1.0 + pre * (1.0 - sigma))
        grads = []
        act[:, x] = active.reshape(C, CY, CZ)
        for y in range(CY):
            span = slice(y * CZ, (y + 1) * CZ)
            piece = (upstream[x, y].astype(F32) * slope[:, span]).astype(BF16)
            grad[y] = piece
            grads.append(piece)
        edges[x] = jnp.where(first_core, grads[CY - 1], grads[0])
        field = total[C : C + RANK] + total[C + RANK : C + 2 * RANK]
        field = field + total[C + 2 * RANK : C + 3 * RANK]
        first, second, third = pieces(field)
        stacked = jnp.concatenate([first, second, third, jnp.ones_like(field)], axis=0)
        joint = joint + lax.dot_general(
            stacked.astype(BF16), jnp.concatenate(grads, axis=1), NT, preferred_element_type=F32
        )
    local = joint[:RANK] + joint[RANK : 2 * RANK] + joint[2 * RANK : 3 * RANK] + base[...]
    both = jnp.concatenate([local, joint[3 * RANK :]], axis=0)
    for copy in range(sums.shape[0]):
        sums[copy] = both


def gradient_kernel(wait, block, upper_out, lower_out, planes, upper, lower, sem):
    low, own_0, own_1, high, across, grad_0, grad_1, error = block
    wait(0, 1, 2, 3, 4)
    fill_planes(planes, low, own_0, own_1, high, across)
    wait(5, 6)
    grads = []
    for grad in (grad_0, grad_1):
        grads.append(jnp.concatenate([grad[y] for y in range(CY)], axis=1))
    wait(7)
    leaving = []
    for pair in range(9):
        span = pl.ds(pair * GROUP, GROUP)
        part = error[:, span]
        for x in range(CX):
            part = part + lax.dot_general(
                grads[x], window(planes, x, pair // 3, pair % 3), NT, preferred_element_type=F32
            )
        rounded = part.astype(BF16)
        upper[:, span] = rounded
        lower[:, span] = (part - rounded.astype(F32)).astype(BF16)
        for side, (held, out) in enumerate(((upper, upper_out), (lower, lower_out))):
            leaving.append(
                pltpu.make_async_copy(held.at[:, span], out.at[:, span], sem.at[2 * pair + side])
            )
            leaving[-1].start()
    for transfer in leaving:
        transfer.wait()


def fold_kernel(parts, copies):
    total = parts[0]
    for source in range(1, parts.shape[0]):
        total = total + parts[source]
    for copy in range(copies.shape[0]):
        copies[copy] = total


def project_kernel(wait, held, parts, factor_p, bias_grad, blocks, *, devices):
    upper, lower = held
    sums = parts[0]
    for source in range(1, parts.shape[0]):
        sums = sums + parts[source]
    bias_grad[...] = sums[RANK : RANK + 1] / devices
    rows = sums[:RANK]
    done = []
    for r in range(RANK):
        vector = rows[r : r + 1]
        vector = vector / jnp.sqrt(jnp.sum(vector * vector, axis=1, keepdims=True) + 1e-06)
        done.append(vector)
        rows = rows - jnp.sum(rows * vector, axis=1, keepdims=True) * vector
    basis = jnp.concatenate(done, axis=0)
    factor_p[...] = basis
    first, second, third = pieces(basis)
    stacked = jnp.concatenate([first, second, third, jnp.zeros_like(basis)], axis=0).astype(BF16)
    wait(0, 1)
    q = lax.dot_general(stacked, upper[...], NN, preferred_element_type=F32)
    q = q + lax.dot_general(stacked, lower[...], NN, preferred_element_type=F32)
    q = q[:RANK] + q[RANK : 2 * RANK] + q[2 * RANK : 3 * RANK]
    for block in range(blocks.shape[0]):
        if block < TAPS:
            blocks[block] = q[:, block * C : (block + 1) * C]
        else:
            blocks[block] = jnp.zeros((RANK, C), F32)


def residual_kernel(wait, held, out, new_error, sem):
    basis, blocks, upper, lower = held
    wait(0, 1, 2, 3)
    leaving = []
    for pair in range(9):
        span = pl.ds(pair * GROUP, GROUP)
        rows = jnp.concatenate([blocks[3 * pair + c] for c in range(3)], axis=1)
        merged = upper[:, span].astype(F32) + lower[:, span].astype(F32)
        new_error[:, span] = merged - lax.dot_general(
            basis[...], rows, TN, precision=HIGHEST, preferred_element_type=F32
        )
        leaving.append(pltpu.make_async_copy(new_error.at[:, span], out.at[:, span], sem.at[pair]))
        leaving[-1].start()
    for transfer in leaving:
        transfer.wait()


def finish_kernel(blocks, factor_q, *, devices):
    for tap in range(TAPS):
        factor_q[:, pl.ds(tap * C, C)] = blocks[tap] / devices


def backward_kernel(wait, held, out, planes):
    low, own_0, own_1, high, middle, weights = held
    wait(0, 1, 2, 3, 4)
    across = (low[CY], middle[0], middle[1], high[CY])
    fill_planes(planes, low, own_0, own_1, high, across)
    wait(5)
    totals = [None] * CX
    for pair in range(9):
        taps = [TAPS - 1 - 3 * pair - c for c in range(3)]
        stack = jnp.concatenate([weights[tap] for tap in taps], axis=0)
        for x in range(CX):
            part = lax.dot_general(
                stack, window(planes, x, pair // 3, pair % 3), TN, preferred_element_type=F32
            )
            totals[x] = part if totals[x] is None else totals[x] + part
    for x in range(CX):
        out[:, x] = totals[x].astype(BF16).reshape(C, CY, CZ)


def pack_kernel(own_0, own_1, middle, down, up):
    for own, row, out in ((own_0, 0, down), (own_1, 1, up)):
        for y in range(CY):
            out[y] = own[y]
        out[CY] = middle[row]


def edge_kernel(low, own_0, own_1, high, edge):
    first = lax.axis_index("sy") == 0
    for xp, source in enumerate((low, own_0, own_1, high)):
        edge[xp] = jnp.where(first, source[CY - 1], source[0])


def swap_cores(edge):
    return lax.ppermute(edge, "sy", [(0, 1), (1, 0)])


def exchange_x(own_0, own_1):
    count = lax.axis_size("sx")
    up = [(i, i + 1) for i in range(count - 1)]
    down = [(i + 1, i) for i in range(count - 1)]
    return lax.ppermute(own_1, "sx", up), lax.ppermute(own_0, "sx", down)


def exchange_y(low, own_0, own_1, high):
    slab = jax.ShapeDtypeStruct((PX, C, CZ), BF16)
    edge = call(edge_kernel, "edge", 2, slab, (low, own_0, own_1, high))
    return swap_cores(edge)


tie = lax.optimization_barrier


def size_of(axes):
    count = 1
    for axis in axes:
        count = count * lax.axis_size(axis)
    return count


def swap(x, axes):
    return lax.all_to_all(x, axes, 0, 0, tiled=True)


def call(kernel, name, room, shapes, args, scratch=(), outs=VMEM):
    return pl.pallas_call(
        kernel,
        out_shape=shapes,
        in_specs=[VMEM] * len(args),
        out_specs=jax.tree.map(lambda _: outs, shapes),
        scratch_shapes=list(scratch),
        compiler_params=pltpu.CompilerParams(vmem_limit_bytes=room * MIB),
        name=name,
    )(*args)


def fetch_and_call(kernel, name, room, shapes, args, scratch=(), outs=VMEM, near=()):
    count = len(args)

    def body(*refs):
        close, refs = refs[: len(near)], refs[len(near) :]
        sources, rest = refs[:count], refs[count:]
        results = len(jax.tree.leaves(shapes))
        held, sem = rest[results : results + count], rest[results + count]
        copies = [
            pltpu.make_async_copy(source, target, sem.at[k])
            for k, (source, target) in enumerate(zip(sources, held))
        ]
        for copy in copies:
            copy.start()

        def wait(*which):
            for k in which:
                copies[k].wait()

        kernel(wait, held, *close, *rest[:results], *rest[results + count + 1 :])

    return pl.pallas_call(
        body,
        out_shape=shapes,
        in_specs=[VMEM] * len(near) + [HBM] * count,
        out_specs=jax.tree.map(lambda _: outs, shapes),
        scratch_shapes=[
            *(pltpu.VMEM(arg.shape, arg.dtype) for arg in args),
            pltpu.SemaphoreType.DMA((count,)),
            *scratch,
        ],
        compiler_params=pltpu.CompilerParams(vmem_limit_bytes=room * MIB),
        name=name,
    )(*near, *args)


def fold(parts, count):
    shape = jax.ShapeDtypeStruct((count,) + parts.shape[1:], F32)
    return call(fold_kernel, "fold", 2, shape, (parts,))


def f32(*shape):
    return jax.ShapeDtypeStruct(shape, F32)


def bf16(*shape):
    return jax.ShapeDtypeStruct(shape, BF16)


def shards(features, cotangent, weights, conv_bias, error_state, warm_factor):
    chips, columns = size_of(DP), size_of(BLOCK)
    devices = chips * columns
    padded = -(-TAPS // columns) * columns
    planes = pltpu.VMEM((GROUP, PX * PY * CZ), BF16)
    error = error_state[0, 0, 0]
    own_0 = jnp.transpose(features[0, :, 0], (1, 0, 2))
    own_1 = jnp.transpose(features[0, :, 1], (1, 0, 2))
    low, high = exchange_x(own_0, own_1)
    upstream = jnp.transpose(cotangent[0], (1, 2, 0, 3))
    lhs, base, bias = call(
        prepare_kernel,
        "prepare",
        8,
        (bf16(C + EXTRA, K), f32(RANK, C), f32(C, C)),
        (weights, warm_factor, error, conv_bias[None]),
    )
    low, high, lhs, base, bias, upstream = tie((low, high, lhs, base, bias, upstream))
    across = exchange_y(low, own_0, own_1, high)
    block = (low, own_0, own_1, high, across)
    act, grad_0, grad_1, edges, sums = call(
        forward_kernel,
        "forward",
        10,
        (
            bf16(C, CX, CY, CZ),
            bf16(CY, C, CZ),
            bf16(CY, C, CZ),
            bf16(CX, C, CZ),
            f32(chips, 2 * RANK, C),
        ),
        (*block, upstream, lhs, bias, base),
        [planes],
    )
    parts = swap(sums, DP)
    upper, lower = fetch_and_call(
        gradient_kernel,
        "gradient",
        60,
        (bf16(C, K), bf16(C, K)),
        (*block, grad_0, grad_1, error),
        [planes, pltpu.VMEM((C, K), BF16), pltpu.VMEM((C, K), BF16), pltpu.SemaphoreType.DMA((18,))],
        HBM,
    )
    parts, upper, lower, edges = tie((parts, upper, lower, edges))
    parts = swap(fold(parts, columns), BLOCK)
    middle = swap_cores(edges)
    factor_p, bias_grad, blocks = fetch_and_call(
        functools.partial(project_kernel, devices=devices),
        "project",
        60,
        (f32(RANK, C), f32(1, C), f32(padded, RANK, C)),
        (upper, lower),
        near=(parts,),
    )
    new_error = fetch_and_call(
        residual_kernel,
        "residual",
        60,
        f32(C, K),
        (factor_p, blocks, upper, lower),
        [pltpu.VMEM((C, K), F32), pltpu.SemaphoreType.DMA((9,))],
        HBM,
    )
    width = padded // columns * RANK
    mine = swap(blocks, BLOCK)
    mine, new_error, middle, near_0, near_1 = tie((mine, new_error, middle, grad_0, grad_1))
    mine = swap(fold(mine.reshape(columns, width, C), chips), DP)
    down, up = call(
        pack_kernel,
        "pack",
        4,
        (bf16(CY + 1, C, CZ), bf16(CY + 1, C, CZ)),
        (near_0, near_1, middle),
    )
    g_low, g_high = exchange_x(down, up)
    mine, g_low, g_high = tie((mine, g_low, g_high))
    blocks = swap(fold(mine, columns), BLOCK).reshape(padded, RANK, C)
    input_grad = fetch_and_call(
        backward_kernel,
        "backward",
        60,
        bf16(C, CX, CY, CZ),
        (g_low, near_0, near_1, g_high, middle, weights),
        [planes],
    )
    factor_q = call(
        functools.partial(finish_kernel, devices=devices), "finish", 2, f32(RANK, K), (blocks,)
    )
    return (
        act[None],
        input_grad[None],
        bias_grad[0],
        factor_p,
        factor_q,
        new_error[None, None, None],
    )


def solution(mesh):
    torus = Mesh(mesh.devices.reshape(4, 8, mesh.shape["sx"], mesh.shape["sy"]), ALL_AXES)
    split = P(DP, None, "sx", "sy", None)
    state = P(DP, "sx", "sy", None, None)
    return jax.shard_map(
        shards,
        mesh=torus,
        in_specs=(split, split, P(), P(), state, P()),
        out_specs=(split, split, P(), P(), P(), state),
        check_vma=False,
    )
```

```python
import functools

import jax
import jax.numpy as jnp
from jax import lax
from jax.experimental import pallas as pl
from jax.experimental.pallas import tpu as pltpu
from jax.sharding import Mesh
from jax.sharding import PartitionSpec as P

DP = ("dp_0", "dp_1")
BLOCK = ("sx", "sy")
ALL_AXES = ("dp_0", "dp_1", "sx", "sy")
C = 128
CX = 2
CY = 4
CZ = 128
PX = CX + 2
PY = CY + 2
TAPS = 27
K = TAPS * C
RANK = 4
GROUP = 3 * C
EXTRA = 4 * RANK
F32 = jnp.float32
BF16 = jnp.bfloat16
NT = (((1,), (1,)), ((), ()))
NN = (((1,), (0,)), ((), ()))
TN = (((0,), (0,)), ((), ()))
HIGHEST = lax.Precision.HIGHEST
VMEM = pl.BlockSpec(memory_space=pltpu.VMEM)
HBM = pl.BlockSpec(memory_space=pltpu.HBM)
MIB = 1024 * 1024


def is_even():
    return lax.rem(lax.axis_index("sx"), 2) == 0


def rows_of(planes, here_a, here_b, from_a, from_b, across):
    even = is_even()
    ascending = (from_b, here_b, here_a, from_a)
    descending = (from_a, here_a, here_b, from_b)
    for xp in range(PX):
        for y in range(CY):
            yield xp, y + 1, jnp.where(even, ascending[xp][y], descending[xp][y])
    first = lax.axis_index("sy") == 0
    for xp in range(PX):
        edge = across(xp)
        nothing = jnp.zeros_like(edge)
        yield xp, 0, jnp.where(first, nothing, edge)
        yield xp, PY - 1, jnp.where(first, edge, nothing)


def fill_planes(planes, *sources):
    lane = lax.broadcasted_iota(jnp.int32, (C, CZ), 1)
    zero = jnp.zeros((C, CZ), F32)
    for xp, yp, block in rows_of(planes, *sources):
        where = pl.ds((xp * PY + yp) * CZ, CZ)
        wide = block.astype(F32)
        before = jnp.where(lane == 0, zero, pltpu.roll(wide, 1, 1))
        after = jnp.where(lane == CZ - 1, zero, pltpu.roll(wide, CZ - 1, 1))
        planes[pl.ds(0, C), where] = before.astype(BF16)
        planes[pl.ds(C, C), where] = block
        planes[pl.ds(2 * C, C), where] = after.astype(BF16)


def window(planes, x, a, b):
    return planes[:, pl.ds(((x + a) * PY + b) * CZ, CY * CZ)]


def convolve(planes, lhs, x):
    total = None
    for a in range(3):
        for b in range(3):
            part = lax.dot_general(
                lhs[:, pl.ds((3 * a + b) * GROUP, GROUP)],
                window(planes, x, a, b),
                NN,
                preferred_element_type=F32,
            )
            total = part if total is None else total + part
    return total


def pieces(x):
    first = x.astype(BF16).astype(F32)
    rest = x - first
    second = rest.astype(BF16).astype(F32)
    third = (rest - second).astype(BF16).astype(F32)
    return first, second, third


def prepare_kernel(weights, warm, error, bias, lhs, base, bias_plane):
    bias_plane[...] = jnp.transpose(jnp.broadcast_to(bias[...], (C, C)))
    for tap in range(TAPS):
        lhs[pl.ds(0, C), pl.ds(tap * C, C)] = weights[tap]
    rows = warm[...]
    first, second, third = pieces(rows)
    stacked = jnp.concatenate([first, second, third, jnp.zeros_like(rows)], axis=0)
    lhs[pl.ds(C, EXTRA), :] = stacked.astype(BF16)
    base[...] = lax.dot_general(rows, error[...], NT, precision=HIGHEST, preferred_element_type=F32)


def forward_kernel(
    wait, held, act_out, grad_a_out, grad_b_out, edges_out, sums_out,
    planes, act, grad_a, grad_b, edges, sums, sem,
):
    here_a, here_b, from_a, from_b, across, upstream, lhs, bias, base = held
    wait(0, 1, 2, 3, 4)
    fill_planes(planes, here_a, here_b, from_a, from_b, lambda xp: across[xp])
    first_core = lax.axis_index("sy") == 0
    even = is_even()
    joint = jnp.zeros((EXTRA, C), F32)
    wait(6, 7, 5)
    cube = []
    leaving = []

    def leave(source, target):
        leaving.append(pltpu.make_async_copy(source, target, sem.at[len(leaving)]))
        leaving[-1].start()

    for x in range(CX):
        total = convolve(planes, lhs, x)
        pre = total[:C] + bias[:, :1]
        sigma = jax.nn.sigmoid(pre)
        active = (pre * sigma).astype(BF16)
        slope = sigma * (1.0 + pre * (1.0 - sigma))
        act[:, x] = active.reshape(C, CY, CZ)
        grads = []
        for y in range(CY):
            span = slice(y * CZ, (y + 1) * CZ)
            grads.append((upstream[x, y].astype(F32) * slope[:, span]).astype(BF16))
        cube.append(grads)
        edges[x] = jnp.where(first_core, grads[CY - 1], grads[0])
        field = total[C : C + RANK] + total[C + RANK : C + 2 * RANK]
        field = field + total[C + 2 * RANK : C + 3 * RANK]
        first, second, third = pieces(field)
        stacked = jnp.concatenate([first, second, third, jnp.ones_like(field)], axis=0)
        joint = joint + lax.dot_general(
            stacked.astype(BF16), jnp.concatenate(grads, axis=1), NT, preferred_element_type=F32
        )
    leave(act, act_out)
    wait(8)
    local = joint[:RANK] + joint[RANK : 2 * RANK] + joint[2 * RANK : 3 * RANK] + base[...]
    both = jnp.concatenate([local, joint[3 * RANK :]], axis=0)
    for copy in range(sums.shape[0]):
        sums[copy] = both
    leave(sums, sums_out)
    for y in range(CY):
        grad_a[y] = jnp.where(even, cube[1][y], cube[0][y])
        grad_b[y] = jnp.where(even, cube[0][y], cube[1][y])
    leave(grad_a, grad_a_out)
    leave(grad_b, grad_b_out)
    leave(edges, edges_out)
    for transfer in leaving:
        transfer.wait()


def gradient_kernel(wait, block, upper_out, lower_out, planes, upper, lower, sem):
    here_a, here_b, from_a, from_b, across, grad_a, grad_b, error = block
    wait(0, 1, 2, 3, 4)
    fill_planes(planes, here_a, here_b, from_a, from_b, lambda xp: across[xp])
    wait(5, 6)
    even = is_even()
    side_a = jnp.concatenate([grad_a[y] for y in range(CY)], axis=1)
    side_b = jnp.concatenate([grad_b[y] for y in range(CY)], axis=1)
    grads = (jnp.where(even, side_b, side_a), jnp.where(even, side_a, side_b))
    wait(7)
    leaving = []
    for pair in range(9):
        span = pl.ds(pair * GROUP, GROUP)
        part = error[:, span]
        for x in range(CX):
            part = part + lax.dot_general(
                grads[x], window(planes, x, pair // 3, pair % 3), NT, preferred_element_type=F32
            )
        rounded = part.astype(BF16)
        upper[:, span] = rounded
        lower[:, span] = (part - rounded.astype(F32)).astype(BF16)
        for side, (held, out) in enumerate(((upper, upper_out), (lower, lower_out))):
            leaving.append(
                pltpu.make_async_copy(held.at[:, span], out.at[:, span], sem.at[2 * pair + side])
            )
            leaving[-1].start()
    for transfer in leaving:
        transfer.wait()


def fold_kernel(parts, copies):
    total = parts[0]
    for source in range(1, parts.shape[0]):
        total = total + parts[source]
    for copy in range(copies.shape[0]):
        copies[copy] = total


def project_kernel(wait, held, parts, factor_p, bias_grad, blocks, *, devices):
    upper, lower = held
    sums = parts[0]
    for source in range(1, parts.shape[0]):
        sums = sums + parts[source]
    bias_grad[...] = sums[RANK : RANK + 1] / devices
    rows = sums[:RANK]
    done = []
    for r in range(RANK):
        vector = rows[r : r + 1]
        vector = vector / jnp.sqrt(jnp.sum(vector * vector, axis=1, keepdims=True) + 1e-06)
        done.append(vector)
        rows = rows - jnp.sum(rows * vector, axis=1, keepdims=True) * vector
    basis = jnp.concatenate(done, axis=0)
    factor_p[...] = basis
    first, second, third = pieces(basis)
    stacked = jnp.concatenate([first, second, third, jnp.zeros_like(basis)], axis=0).astype(BF16)
    wait(0, 1)
    q = lax.dot_general(stacked, upper[...], NN, preferred_element_type=F32)
    q = q + lax.dot_general(stacked, lower[...], NN, preferred_element_type=F32)
    q = q[:RANK] + q[RANK : 2 * RANK] + q[2 * RANK : 3 * RANK]
    for block in range(blocks.shape[0]):
        if block < TAPS:
            blocks[block] = q[:, block * C : (block + 1) * C]
        else:
            blocks[block] = jnp.zeros((RANK, C), F32)


def residual_kernel(wait, held, out, new_error, sem):
    basis, blocks, upper, lower = held
    wait(0, 1)
    b1, b2, b3 = pieces(basis[...])
    left = jnp.concatenate([b1, b2, b3, b1, b2, b1], axis=0).astype(BF16)
    q = jnp.concatenate([blocks[tap] for tap in range(TAPS)], axis=1)
    q1, q2, q3 = pieces(q)
    right = jnp.concatenate([q1, q1, q1, q2, q2, q3], axis=0).astype(BF16)
    wait(2, 3)
    leaving = []
    for pair in range(9):
        span = pl.ds(pair * GROUP, GROUP)
        merged = upper[:, span].astype(F32) + lower[:, span].astype(F32)
        new_error[:, span] = merged - lax.dot_general(
            left, right[:, pair * GROUP : (pair + 1) * GROUP], TN, preferred_element_type=F32
        )
        leaving.append(pltpu.make_async_copy(new_error.at[:, span], out.at[:, span], sem.at[pair]))
        leaving[-1].start()
    for transfer in leaving:
        transfer.wait()


def finish_kernel(blocks, factor_q, *, devices):
    for tap in range(TAPS):
        factor_q[:, pl.ds(tap * C, C)] = blocks[tap] / devices


def backward_kernel(wait, held, out, planes):
    here_a, here_b, from_a, from_b, middle, weights = held
    wait(0, 1, 2, 3, 4)
    even = is_even()

    def across(xp):
        if 0 < xp < PX - 1:
            return middle[xp - 1]
        above = xp > 0
        return jnp.where(even == above, from_a[CY], from_b[CY])

    fill_planes(planes, here_a, here_b, from_a, from_b, across)
    wait(5)
    totals = [None] * CX
    for pair in range(9):
        taps = [TAPS - 1 - 3 * pair - c for c in range(3)]
        stack = jnp.concatenate([weights[tap] for tap in taps], axis=0)
        for x in range(CX):
            part = lax.dot_general(
                stack, window(planes, x, pair // 3, pair % 3), TN, preferred_element_type=F32
            )
            totals[x] = part if totals[x] is None else totals[x] + part
    for x in range(CX):
        out[:, x] = totals[x].astype(BF16).reshape(C, CY, CZ)


def pack_kernel(here_a, here_b, middle, to_a, to_b):
    even = is_even()
    for y in range(CY):
        to_a[y] = here_a[y]
        to_b[y] = here_b[y]
    to_a[CY] = jnp.where(even, middle[1], middle[0])
    to_b[CY] = jnp.where(even, middle[0], middle[1])


def edge_kernel(here_a, here_b, from_a, from_b, edge):
    first = lax.axis_index("sy") == 0
    even = is_even()
    ascending = (from_b, here_b, here_a, from_a)
    descending = (from_a, here_a, here_b, from_b)
    for xp in range(PX):
        last = jnp.where(even, ascending[xp][CY - 1], descending[xp][CY - 1])
        start = jnp.where(even, ascending[xp][0], descending[xp][0])
        edge[xp] = jnp.where(first, last, start)


def swap_cores(edge):
    return lax.ppermute(edge, "sy", [(0, 1), (1, 0)])


def exchange_x(to_a, to_b):
    count = lax.axis_size("sx")
    pairs_a = [(i, i ^ 1) for i in range(count) if i ^ 1 < count]
    pairs_b = [(i, j) for i in range(1, count - 1) for j in [((i - 1) ^ 1) + 1] if j < count]
    return lax.ppermute(to_a, "sx", pairs_a), lax.ppermute(to_b, "sx", pairs_b)


tie = lax.optimization_barrier


def size_of(axes):
    count = 1
    for axis in axes:
        count = count * lax.axis_size(axis)
    return count


def swap(x, axes):
    return lax.all_to_all(x, axes, 0, 0, tiled=True)


def call(kernel, name, room, shapes, args, scratch=(), outs=VMEM):
    return pl.pallas_call(
        kernel,
        out_shape=shapes,
        in_specs=[VMEM] * len(args),
        out_specs=jax.tree.map(lambda _: outs, shapes),
        scratch_shapes=list(scratch),
        compiler_params=pltpu.CompilerParams(vmem_limit_bytes=room * MIB),
        name=name,
    )(*args)


def fetch_and_call(kernel, name, room, shapes, args, scratch=(), outs=VMEM, near=()):
    count = len(args)

    def body(*refs):
        close, refs = refs[: len(near)], refs[len(near) :]
        sources, rest = refs[:count], refs[count:]
        results = len(jax.tree.leaves(shapes))
        held, sem = rest[results : results + count], rest[results + count]
        copies = [
            pltpu.make_async_copy(source, target, sem.at[k])
            for k, (source, target) in enumerate(zip(sources, held))
        ]
        for copy in copies:
            copy.start()

        def wait(*which):
            for k in which:
                copies[k].wait()

        kernel(wait, held, *close, *rest[:results], *rest[results + count + 1 :])

    return pl.pallas_call(
        body,
        out_shape=shapes,
        in_specs=[VMEM] * len(near) + [HBM] * count,
        out_specs=jax.tree.map(lambda _: outs, shapes),
        scratch_shapes=[
            *(pltpu.VMEM(arg.shape, arg.dtype) for arg in args),
            pltpu.SemaphoreType.DMA((count,)),
            *scratch,
        ],
        compiler_params=pltpu.CompilerParams(vmem_limit_bytes=room * MIB),
        name=name,
    )(*near, *args)


def fold(parts, count):
    shape = jax.ShapeDtypeStruct((count,) + parts.shape[1:], F32)
    return call(fold_kernel, "fold", 2, shape, (parts,))


def f32(*shape):
    return jax.ShapeDtypeStruct(shape, F32)


def bf16(*shape):
    return jax.ShapeDtypeStruct(shape, BF16)


def shards(features, cotangent, weights, conv_bias, error_state, warm_factor):
    chips, columns = size_of(DP), size_of(BLOCK)
    devices = chips * columns
    padded = -(-TAPS // columns) * columns
    planes = pltpu.VMEM((GROUP, PX * PY * CZ), BF16)
    error = error_state[0, 0, 0]
    shift = jnp.where(is_even(), 1, 0)
    here_a, here_b = (
        jnp.transpose(lax.dynamic_index_in_dim(features[0], which, 1, False), (1, 0, 2))
        for which in (shift, 1 - shift)
    )
    from_a, from_b = exchange_x(here_a, here_b)
    upstream = jnp.transpose(cotangent[0], (1, 2, 0, 3))
    lhs, base, bias = call(
        prepare_kernel,
        "prepare",
        8,
        (bf16(C + EXTRA, K), f32(RANK, C), f32(C, C)),
        (weights, warm_factor, error, conv_bias[None]),
    )
    from_a, from_b, lhs, base, bias, upstream = tie((from_a, from_b, lhs, base, bias, upstream))
    edge = call(edge_kernel, "edge", 2, bf16(PX, C, CZ), (here_a, here_b, from_a, from_b))
    block = (here_a, here_b, from_a, from_b, swap_cores(edge))
    shapes = (
        bf16(C, CX, CY, CZ),
        bf16(CY, C, CZ),
        bf16(CY, C, CZ),
        bf16(CX, C, CZ),
        f32(chips, 2 * RANK, C),
    )
    act, grad_a, grad_b, edges, sums = fetch_and_call(
        forward_kernel,
        "forward",
        60,
        shapes,
        (*block, upstream, lhs, bias, base),
        [planes, *(pltpu.VMEM(s.shape, s.dtype) for s in shapes), pltpu.SemaphoreType.DMA((5,))],
        HBM,
    )
    parts = swap(sums, DP)
    upper, lower = fetch_and_call(
        gradient_kernel,
        "gradient",
        60,
        (bf16(C, K), bf16(C, K)),
        (*block, grad_a, grad_b, error),
        [planes, pltpu.VMEM((C, K), BF16), pltpu.VMEM((C, K), BF16), pltpu.SemaphoreType.DMA((18,))],
        HBM,
    )
    parts, upper, lower, edges = tie((parts, upper, lower, edges))
    parts = swap(fold(parts, columns), BLOCK)
    parts, middle = tie((parts, swap_cores(edges)))
    factor_p, bias_grad, blocks = fetch_and_call(
        functools.partial(project_kernel, devices=devices),
        "project",
        60,
        (f32(RANK, C), f32(1, C), f32(padded, RANK, C)),
        (upper, lower),
        near=(parts,),
    )
    new_error = fetch_and_call(
        residual_kernel,
        "residual",
        60,
        f32(C, K),
        (factor_p, blocks, upper, lower),
        [pltpu.VMEM((C, K), F32), pltpu.SemaphoreType.DMA((9,))],
        HBM,
    )
    width = padded // columns * RANK
    mine = swap(blocks, BLOCK)
    mine, new_error, middle, near_a, near_b = tie((mine, new_error, middle, grad_a, grad_b))
    mine = swap(fold(mine.reshape(columns, width, C), chips), DP)
    to_a, to_b = call(
        pack_kernel,
        "pack",
        4,
        (bf16(CY + 1, C, CZ), bf16(CY + 1, C, CZ)),
        (near_a, near_b, middle),
    )
    g_from_a, g_from_b = exchange_x(to_a, to_b)
    blocks = swap(fold(mine, columns), BLOCK).reshape(padded, RANK, C)
    input_grad = fetch_and_call(
        backward_kernel,
        "backward",
        60,
        bf16(C, CX, CY, CZ),
        (near_a, near_b, g_from_a, g_from_b, middle, weights),
        [planes],
    )
    factor_q = call(
        functools.partial(finish_kernel, devices=devices), "finish", 2, f32(RANK, K), (blocks,)
    )
    return (
        act[None],
        input_grad[None],
        bias_grad[0],
        factor_p,
        factor_q,
        new_error[None, None, None],
    )


def solution(mesh):
    torus = Mesh(mesh.devices.reshape(4, 8, mesh.shape["sx"], mesh.shape["sy"]), ALL_AXES)
    split = P(DP, None, "sx", "sy", None)
    state = P(DP, "sx", "sy", None, None)
    return jax.shard_map(
        shards,
        mesh=torus,
        in_specs=(split, split, P(), P(), state, P()),
        out_specs=(split, split, P(), P(), P(), state),
        check_vma=False,
    )
```

```python
import functools

import jax
import jax.numpy as jnp
from jax import lax
from jax.experimental import pallas as pl
from jax.experimental.pallas import tpu as pltpu
from jax.sharding import Mesh
from jax.sharding import PartitionSpec as P

DP = ("dp_0", "dp_1")
BLOCK = ("sx", "sy")
ALL_AXES = ("dp_0", "dp_1", "sx", "sy")
C = 128
CX = 2
CY = 4
CZ = 128
PX = CX + 2
PY = CY + 2
TAPS = 27
K = TAPS * C
RANK = 4
GROUP = 3 * C
EXTRA = 4 * RANK
F32 = jnp.float32
BF16 = jnp.bfloat16
NT = (((1,), (1,)), ((), ()))
NN = (((1,), (0,)), ((), ()))
TN = (((0,), (0,)), ((), ()))
HIGHEST = lax.Precision.HIGHEST
VMEM = pl.BlockSpec(memory_space=pltpu.VMEM)
HBM = pl.BlockSpec(memory_space=pltpu.HBM)
MIB = 1024 * 1024


def is_even():
    return lax.rem(lax.axis_index("sx"), 2) == 0


def rows_of(planes, here_a, here_b, from_a, from_b, across):
    even = is_even()
    ascending = (from_b, here_b, here_a, from_a)
    descending = (from_a, here_a, here_b, from_b)
    for xp in range(PX):
        for y in range(CY):
            yield xp, y + 1, jnp.where(even, ascending[xp][y], descending[xp][y])
    first = lax.axis_index("sy") == 0
    for xp in range(PX):
        edge = across(xp)
        nothing = jnp.zeros_like(edge)
        yield xp, 0, jnp.where(first, nothing, edge)
        yield xp, PY - 1, jnp.where(first, edge, nothing)


def fill_planes(planes, *sources):
    lane = lax.broadcasted_iota(jnp.int32, (C, CZ), 1)
    zero = jnp.zeros((C, CZ), F32)
    for xp, yp, block in rows_of(planes, *sources):
        where = pl.ds((xp * PY + yp) * CZ, CZ)
        wide = block.astype(F32)
        before = jnp.where(lane == 0, zero, pltpu.roll(wide, 1, 1))
        after = jnp.where(lane == CZ - 1, zero, pltpu.roll(wide, CZ - 1, 1))
        planes[pl.ds(0, C), where] = before.astype(BF16)
        planes[pl.ds(C, C), where] = block
        planes[pl.ds(2 * C, C), where] = after.astype(BF16)


def window(planes, x, a, b):
    return planes[:, pl.ds(((x + a) * PY + b) * CZ, CY * CZ)]


def pieces(x):
    first = x.astype(BF16).astype(F32)
    rest = x - first
    second = rest.astype(BF16).astype(F32)
    third = (rest - second).astype(BF16).astype(F32)
    return first, second, third


def relayout_kernel(cube, here_a, here_b, edges, edge_a, edge_b):
    even = is_even()
    first_core = lax.axis_index("sy") == 0
    flat = [cube[:, x].reshape(C, CY * CZ) for x in range(CX)]
    rows = [[flat[x][:, y * CZ : (y + 1) * CZ] for y in range(CY)] for x in range(CX)]
    for y in range(CY):
        here_a[y] = jnp.where(even, rows[1][y], rows[0][y])
        here_b[y] = jnp.where(even, rows[0][y], rows[1][y])
    border = [jnp.where(first_core, rows[x][CY - 1], rows[x][0]) for x in range(CX)]
    for x in range(CX):
        edges[x] = border[x]
    edge_a[0] = jnp.where(even, border[1], border[0])
    edge_b[0] = jnp.where(even, border[0], border[1])


def base_kernel(warm, error, base):
    base[...] = lax.dot_general(
        warm[...], error[...], NT, precision=HIGHEST, preferred_element_type=F32
    )


def rows_across(middle, corner_a, corner_b):
    even = is_even()

    def across(xp):
        if 0 < xp < PX - 1:
            return middle[xp - 1]
        return jnp.where(even == (xp > 0), corner_a, corner_b)

    return across


def forward_kernel(
    here_a, here_b, from_a, from_b, middle, corner_a, corner_b,
    upstream, weights, warm, bias, base,
    act, grad_a, grad_b, edges, sums, planes,
):
    across = rows_across(middle, corner_a[0], corner_b[0])
    fill_planes(planes, here_a, here_b, from_a, from_b, across)
    first_core = lax.axis_index("sy") == 0
    even = is_even()
    offset = jnp.transpose(jnp.broadcast_to(bias[...], (C, C)))[:, :1]
    rows = warm[...]
    terms = jnp.concatenate([*pieces(rows), jnp.zeros_like(rows)], axis=0).astype(BF16)
    totals = [None] * CX
    for pair in range(9):
        stack = jnp.concatenate([weights[3 * pair + c] for c in range(3)], axis=1)
        span = slice(pair * GROUP, (pair + 1) * GROUP)
        stack = jnp.concatenate([stack, terms[:, span]], axis=0)
        for x in range(CX):
            part = lax.dot_general(
                stack, window(planes, x, pair // 3, pair % 3), NN, preferred_element_type=F32
            )
            totals[x] = part if totals[x] is None else totals[x] + part
    joint = jnp.zeros((EXTRA, C), F32)
    cube = []
    for x in range(CX):
        total = totals[x]
        pre = total[:C] + offset
        sigma = jax.nn.sigmoid(pre)
        slope = sigma * (1.0 + pre * (1.0 - sigma))
        act[:, x] = (pre * sigma).astype(BF16).reshape(C, CY, CZ)
        above = upstream[:, x].reshape(C, CY * CZ).astype(F32)
        gradient = (above * slope).astype(BF16)
        grads = [gradient[:, y * CZ : (y + 1) * CZ] for y in range(CY)]
        cube.append(grads)
        edges[x] = jnp.where(first_core, grads[CY - 1], grads[0])
        field = total[C : C + RANK] + total[C + RANK : C + 2 * RANK]
        field = field + total[C + 2 * RANK : C + 3 * RANK]
        stacked = jnp.concatenate([*pieces(field), jnp.ones_like(field)], axis=0)
        joint = joint + lax.dot_general(
            stacked.astype(BF16), gradient, NT, preferred_element_type=F32
        )
    local = joint[:RANK] + joint[RANK : 2 * RANK] + joint[2 * RANK : 3 * RANK] + base[...]
    both = jnp.concatenate([local, joint[3 * RANK :]], axis=0)
    for copy in range(sums.shape[0]):
        sums[copy] = both
    for y in range(CY):
        grad_a[y] = jnp.where(even, cube[1][y], cube[0][y])
        grad_b[y] = jnp.where(even, cube[0][y], cube[1][y])


def gradient_kernel(wait, block, upper_out, lower_out, planes, upper, lower, sem):
    here_a, here_b, from_a, from_b, middle, corner_a, corner_b, grad_a, grad_b, error = block
    wait(0, 1, 2, 3, 4, 5, 6)
    across = rows_across(middle, corner_a[0], corner_b[0])
    fill_planes(planes, here_a, here_b, from_a, from_b, across)
    wait(7, 8)
    even = is_even()
    side_a = jnp.concatenate([grad_a[y] for y in range(CY)], axis=1)
    side_b = jnp.concatenate([grad_b[y] for y in range(CY)], axis=1)
    grads = (jnp.where(even, side_b, side_a), jnp.where(even, side_a, side_b))
    wait(9)
    leaving = []
    for pair in range(9):
        span = pl.ds(pair * GROUP, GROUP)
        part = error[:, span]
        for x in range(CX):
            part = part + lax.dot_general(
                grads[x], window(planes, x, pair // 3, pair % 3), NT, preferred_element_type=F32
            )
        rounded = part.astype(BF16)
        upper[:, span] = rounded
        lower[:, span] = (part - rounded.astype(F32)).astype(BF16)
        for side, (held, out) in enumerate(((upper, upper_out), (lower, lower_out))):
            leaving.append(
                pltpu.make_async_copy(held.at[:, span], out.at[:, span], sem.at[2 * pair + side])
            )
            leaving[-1].start()
    for transfer in leaving:
        transfer.wait()


def fold_kernel(parts, copies):
    total = parts[0]
    for source in range(1, parts.shape[0]):
        total = total + parts[source]
    for copy in range(copies.shape[0]):
        copies[copy] = total


def project_kernel(wait, held, parts, factor_p, bias_grad, blocks, *, devices):
    upper, lower = held
    sums = parts[0]
    for source in range(1, parts.shape[0]):
        sums = sums + parts[source]
    bias_grad[...] = sums[RANK : RANK + 1] / devices
    rows = sums[:RANK]
    done = []
    for r in range(RANK):
        vector = rows[r : r + 1]
        vector = vector / jnp.sqrt(jnp.sum(vector * vector, axis=1, keepdims=True) + 1e-06)
        done.append(vector)
        rows = rows - jnp.sum(rows * vector, axis=1, keepdims=True) * vector
    basis = jnp.concatenate(done, axis=0)
    factor_p[...] = basis
    first, second, third = pieces(basis)
    stacked = jnp.concatenate([first, second, third, jnp.zeros_like(basis)], axis=0).astype(BF16)
    wait(0, 1)
    q = lax.dot_general(stacked, upper[...], NN, preferred_element_type=F32)
    q = q + lax.dot_general(stacked, lower[...], NN, preferred_element_type=F32)
    q = q[:RANK] + q[RANK : 2 * RANK] + q[2 * RANK : 3 * RANK]
    for block in range(blocks.shape[0]):
        if block < TAPS:
            blocks[block] = q[:, block * C : (block + 1) * C]
        else:
            blocks[block] = jnp.zeros((RANK, C), F32)


def residual_kernel(wait, held, out, new_error, sem):
    basis, blocks, upper, lower = held
    wait(0, 1)
    b1, b2, b3 = pieces(basis[...])
    left = jnp.concatenate([b1, b2, b3, b1, b2, b1], axis=0).astype(BF16)
    q = jnp.concatenate([blocks[tap] for tap in range(TAPS)], axis=1)
    q1, q2, q3 = pieces(q)
    right = jnp.concatenate([q1, q1, q1, q2, q2, q3], axis=0).astype(BF16)
    wait(2, 3)
    leaving = []
    for pair in range(9):
        span = pl.ds(pair * GROUP, GROUP)
        merged = upper[:, span].astype(F32) + lower[:, span].astype(F32)
        new_error[:, span] = merged - lax.dot_general(
            left, right[:, pair * GROUP : (pair + 1) * GROUP], TN, preferred_element_type=F32
        )
        leaving.append(pltpu.make_async_copy(new_error.at[:, span], out.at[:, span], sem.at[pair]))
        leaving[-1].start()
    for transfer in leaving:
        transfer.wait()


def finish_kernel(blocks, factor_q, *, devices):
    for tap in range(TAPS):
        factor_q[:, pl.ds(tap * C, C)] = blocks[tap] / devices


def backward_kernel(wait, held, out, planes):
    here_a, here_b, from_a, from_b, middle, weights = held
    wait(0, 1, 2, 3, 4)
    across = rows_across(middle, from_a[CY], from_b[CY])
    fill_planes(planes, here_a, here_b, from_a, from_b, across)
    wait(5)
    totals = [None] * CX
    for pair in range(9):
        taps = [TAPS - 1 - 3 * pair - c for c in range(3)]
        stack = jnp.concatenate([weights[tap] for tap in taps], axis=0)
        for x in range(CX):
            part = lax.dot_general(
                stack, window(planes, x, pair // 3, pair % 3), TN, preferred_element_type=F32
            )
            totals[x] = part if totals[x] is None else totals[x] + part
    for x in range(CX):
        out[:, x] = totals[x].astype(BF16).reshape(C, CY, CZ)


def pack_kernel(here_a, here_b, middle, to_a, to_b):
    even = is_even()
    for y in range(CY):
        to_a[y] = here_a[y]
        to_b[y] = here_b[y]
    to_a[CY] = jnp.where(even, middle[1], middle[0])
    to_b[CY] = jnp.where(even, middle[0], middle[1])


def swap_cores(edge):
    return lax.ppermute(edge, "sy", [(0, 1), (1, 0)])


def pairs_of(count):
    pairs_a = [(i, i ^ 1) for i in range(count) if i ^ 1 < count]
    pairs_b = [(i, j) for i in range(1, count) for j in [((i - 1) ^ 1) + 1] if j < count]
    return pairs_a, pairs_b


def exchange_x(to_a, to_b):
    pairs_a, pairs_b = pairs_of(lax.axis_size("sx"))
    return lax.ppermute(to_a, "sx", pairs_a), lax.ppermute(to_b, "sx", pairs_b)


def exchange_corners(to_a, to_b):
    cores = lax.axis_size("sy")
    both = [
        [(i * cores + c, j * cores + 1 - c) for i, j in pairs for c in range(cores)]
        for pairs in pairs_of(lax.axis_size("sx"))
    ]
    return lax.ppermute(to_a, BLOCK, both[0]), lax.ppermute(to_b, BLOCK, both[1])


tie = lax.optimization_barrier


def size_of(axes):
    count = 1
    for axis in axes:
        count = count * lax.axis_size(axis)
    return count


def swap(x, axes):
    return lax.all_to_all(x, axes, 0, 0, tiled=True)


def call(kernel, name, room, shapes, args, scratch=(), outs=VMEM):
    return pl.pallas_call(
        kernel,
        out_shape=shapes,
        in_specs=[VMEM] * len(args),
        out_specs=jax.tree.map(lambda _: outs, shapes),
        scratch_shapes=list(scratch),
        compiler_params=pltpu.CompilerParams(vmem_limit_bytes=room * MIB),
        name=name,
    )(*args)


def fetch_and_call(kernel, name, room, shapes, args, scratch=(), outs=VMEM, near=()):
    count = len(args)

    def body(*refs):
        close, refs = refs[: len(near)], refs[len(near) :]
        sources, rest = refs[:count], refs[count:]
        results = len(jax.tree.leaves(shapes))
        held, sem = rest[results : results + count], rest[results + count]
        copies = [
            pltpu.make_async_copy(source, target, sem.at[k])
            for k, (source, target) in enumerate(zip(sources, held))
        ]
        for copy in copies:
            copy.start()

        def wait(*which):
            for k in which:
                copies[k].wait()

        kernel(wait, held, *close, *rest[:results], *rest[results + count + 1 :])

    return pl.pallas_call(
        body,
        out_shape=shapes,
        in_specs=[VMEM] * len(near) + [HBM] * count,
        out_specs=jax.tree.map(lambda _: outs, shapes),
        scratch_shapes=[
            *(pltpu.VMEM(arg.shape, arg.dtype) for arg in args),
            pltpu.SemaphoreType.DMA((count,)),
            *scratch,
        ],
        compiler_params=pltpu.CompilerParams(vmem_limit_bytes=room * MIB),
        name=name,
    )(*near, *args)


def fold(parts, count):
    shape = jax.ShapeDtypeStruct((count,) + parts.shape[1:], F32)
    return call(fold_kernel, "fold", 2, shape, (parts,))


def f32(*shape):
    return jax.ShapeDtypeStruct(shape, F32)


def bf16(*shape):
    return jax.ShapeDtypeStruct(shape, BF16)


def shards(features, cotangent, weights, conv_bias, error_state, warm_factor):
    chips, columns = size_of(DP), size_of(BLOCK)
    devices = chips * columns
    padded = -(-TAPS // columns) * columns
    planes = pltpu.VMEM((GROUP, PX * PY * CZ), BF16)
    error = error_state[0, 0, 0]
    here_a, here_b, edges, edge_a, edge_b = call(
        relayout_kernel,
        "relayout",
        4,
        (bf16(CY, C, CZ), bf16(CY, C, CZ), bf16(CX, C, CZ), bf16(1, C, CZ), bf16(1, C, CZ)),
        (features[0],),
    )
    from_a, from_b = exchange_x(here_a, here_b)
    corner_a, corner_b = exchange_corners(edge_a, edge_b)
    middle = swap_cores(edges)
    base = call(base_kernel, "base", 4, f32(RANK, C), (warm_factor, error))
    from_a, from_b, base = tie((from_a, from_b, base))
    block = (here_a, here_b, from_a, from_b, middle, corner_a, corner_b)
    act, grad_a, grad_b, edges, sums = call(
        forward_kernel,
        "forward",
        12,
        (
            bf16(C, CX, CY, CZ),
            bf16(CY, C, CZ),
            bf16(CY, C, CZ),
            bf16(CX, C, CZ),
            f32(chips, 2 * RANK, C),
        ),
        (*block, cotangent[0], weights, warm_factor, conv_bias[None], base),
        [planes],
    )
    parts = swap(sums, DP)
    upper, lower = fetch_and_call(
        gradient_kernel,
        "gradient",
        60,
        (bf16(C, K), bf16(C, K)),
        (*block, grad_a, grad_b, error),
        [planes, pltpu.VMEM((C, K), BF16), pltpu.VMEM((C, K), BF16), pltpu.SemaphoreType.DMA((18,))],
        HBM,
    )
    parts, upper, lower, edges = tie((parts, upper, lower, edges))
    parts = swap(fold(parts, columns), BLOCK)
    parts, middle = tie((parts, swap_cores(edges)))
    factor_p, bias_grad, blocks = fetch_and_call(
        functools.partial(project_kernel, devices=devices),
        "project",
        60,
        (f32(RANK, C), f32(1, C), f32(padded, RANK, C)),
        (upper, lower),
        near=(parts,),
    )
    new_error = fetch_and_call(
        residual_kernel,
        "residual",
        60,
        f32(C, K),
        (factor_p, blocks, upper, lower),
        [pltpu.VMEM((C, K), F32), pltpu.SemaphoreType.DMA((9,))],
        HBM,
    )
    width = padded // columns * RANK
    mine = swap(blocks, BLOCK)
    mine, new_error, middle, near_a, near_b = tie((mine, new_error, middle, grad_a, grad_b))
    mine = swap(fold(mine.reshape(columns, width, C), chips), DP)
    to_a, to_b = call(
        pack_kernel,
        "pack",
        4,
        (bf16(CY + 1, C, CZ), bf16(CY + 1, C, CZ)),
        (near_a, near_b, middle),
    )
    g_from_a, g_from_b = exchange_x(to_a, to_b)
    blocks = swap(fold(mine, columns), BLOCK).reshape(padded, RANK, C)
    input_grad = fetch_and_call(
        backward_kernel,
        "backward",
        60,
        bf16(C, CX, CY, CZ),
        (near_a, near_b, g_from_a, g_from_b, middle, weights),
        [planes],
    )
    factor_q = call(
        functools.partial(finish_kernel, devices=devices), "finish", 2, f32(RANK, K), (blocks,)
    )
    return (
        act[None],
        input_grad[None],
        bias_grad[0],
        factor_p,
        factor_q,
        new_error[None, None, None],
    )


def solution(mesh):
    torus = Mesh(mesh.devices.reshape(4, 8, mesh.shape["sx"], mesh.shape["sy"]), ALL_AXES)
    split = P(DP, None, "sx", "sy", None)
    state = P(DP, "sx", "sy", None, None)
    return jax.shard_map(
        shards,
        mesh=torus,
        in_specs=(split, split, P(), P(), state, P()),
        out_specs=(split, split, P(), P(), P(), state),
        check_vma=False,
    )
```

```python
import functools

import jax
import jax.numpy as jnp
from jax import lax
from jax.experimental import pallas as pl
from jax.experimental.pallas import tpu as pltpu
from jax.sharding import Mesh
from jax.sharding import PartitionSpec as P

DP = ("dp_0", "dp_1")
BLOCK = ("sx", "sy")
ALL_AXES = ("dp_0", "dp_1", "sx", "sy")
C = 128
CX = 2
CY = 4
CZ = 128
PX = CX + 2
PY = CY + 2
TAPS = 27
K = TAPS * C
RANK = 4
GROUP = 3 * C
EXTRA = 4 * RANK
F32 = jnp.float32
BF16 = jnp.bfloat16
NT = (((1,), (1,)), ((), ()))
NN = (((1,), (0,)), ((), ()))
TN = (((0,), (0,)), ((), ()))
HIGHEST = lax.Precision.HIGHEST
VMEM = pl.BlockSpec(memory_space=pltpu.VMEM)
HBM = pl.BlockSpec(memory_space=pltpu.HBM)
MIB = 1024 * 1024


def is_even():
    return lax.rem(lax.axis_index("sx"), 2) == 0


def rows_of(planes, here_a, here_b, from_a, from_b, across):
    even = is_even()
    ascending = (from_b, here_b, here_a, from_a)
    descending = (from_a, here_a, here_b, from_b)
    for xp in range(PX):
        for y in range(CY):
            yield xp, y + 1, jnp.where(even, ascending[xp][y], descending[xp][y])
    first = lax.axis_index("sy") == 0
    for xp in range(PX):
        edge = across(xp)
        nothing = jnp.zeros_like(edge)
        yield xp, 0, jnp.where(first, nothing, edge)
        yield xp, PY - 1, jnp.where(first, edge, nothing)


def fill_planes(planes, *sources):
    lane = lax.broadcasted_iota(jnp.int32, (C, CZ), 1)
    zero = jnp.zeros((C, CZ), F32)
    for xp, yp, block in rows_of(planes, *sources):
        where = pl.ds((xp * PY + yp) * CZ, CZ)
        wide = block.astype(F32)
        before = jnp.where(lane == 0, zero, pltpu.roll(wide, 1, 1))
        after = jnp.where(lane == CZ - 1, zero, pltpu.roll(wide, CZ - 1, 1))
        planes[pl.ds(0, C), where] = before.astype(BF16)
        planes[pl.ds(C, C), where] = block
        planes[pl.ds(2 * C, C), where] = after.astype(BF16)


def window(planes, x, a, b):
    return planes[:, pl.ds(((x + a) * PY + b) * CZ, CY * CZ)]


def pieces(x):
    first = x.astype(BF16).astype(F32)
    rest = x - first
    second = rest.astype(BF16).astype(F32)
    third = (rest - second).astype(BF16).astype(F32)
    return first, second, third


def relayout_kernel(cube, here_a, here_b):
    even = is_even()
    flat = [cube[:, x].reshape(C, CY * CZ) for x in range(CX)]
    for y in range(CY):
        low, high = (flat[x][:, y * CZ : (y + 1) * CZ] for x in range(CX))
        here_a[y] = jnp.where(even, high, low)
        here_b[y] = jnp.where(even, low, high)


def edge_kernel(here_a, here_b, from_a, from_b, edge):
    first = lax.axis_index("sy") == 0
    even = is_even()
    border = [jnp.where(first, plane[CY - 1], plane[0]) for plane in (here_a, here_b, from_a, from_b)]
    edge[0] = jnp.where(even, border[1], border[0])
    edge[1] = jnp.where(even, border[0], border[1])
    edge[2] = border[2]
    edge[3] = border[3]


def base_kernel(warm, error, base):
    base[...] = lax.dot_general(
        warm[...], error[...], NT, precision=HIGHEST, preferred_element_type=F32
    )


def rows_across(middle, corner_a, corner_b):
    even = is_even()

    def across(xp):
        if 0 < xp < PX - 1:
            return middle[xp - 1]
        return jnp.where(even == (xp > 0), corner_a, corner_b)

    return across


def forward_kernel(
    here_a, here_b, from_a, from_b, middle, upstream,
    weights, warm, bias, base,
    act, grad_a, grad_b, edges, sums, planes,
):
    across = rows_across(middle, middle[2], middle[3])
    fill_planes(planes, here_a, here_b, from_a, from_b, across)
    first_core = lax.axis_index("sy") == 0
    even = is_even()
    offset = jnp.transpose(jnp.broadcast_to(bias[...], (C, C)))[:, :1]
    rows = warm[...]
    terms = jnp.concatenate([*pieces(rows), jnp.zeros_like(rows)], axis=0).astype(BF16)
    totals = [None] * CX
    for pair in range(9):
        stack = jnp.concatenate([weights[3 * pair + c] for c in range(3)], axis=1)
        span = slice(pair * GROUP, (pair + 1) * GROUP)
        stack = jnp.concatenate([stack, terms[:, span]], axis=0)
        for x in range(CX):
            part = lax.dot_general(
                stack, window(planes, x, pair // 3, pair % 3), NN, preferred_element_type=F32
            )
            totals[x] = part if totals[x] is None else totals[x] + part
    joint = jnp.zeros((EXTRA, C), F32)
    cube = []
    for x in range(CX):
        total = totals[x]
        pre = total[:C] + offset
        sigma = jax.nn.sigmoid(pre)
        slope = sigma * (1.0 + pre * (1.0 - sigma))
        act[:, x] = (pre * sigma).astype(BF16).reshape(C, CY, CZ)
        above = upstream[:, x].reshape(C, CY * CZ).astype(F32)
        gradient = (above * slope).astype(BF16)
        grads = [gradient[:, y * CZ : (y + 1) * CZ] for y in range(CY)]
        cube.append(grads)
        edges[x] = jnp.where(first_core, grads[CY - 1], grads[0])
        field = total[C : C + RANK] + total[C + RANK : C + 2 * RANK]
        field = field + total[C + 2 * RANK : C + 3 * RANK]
        stacked = jnp.concatenate([*pieces(field), jnp.ones_like(field)], axis=0)
        joint = joint + lax.dot_general(
            stacked.astype(BF16), gradient, NT, preferred_element_type=F32
        )
    local = joint[:RANK] + joint[RANK : 2 * RANK] + joint[2 * RANK : 3 * RANK] + base[...]
    both = jnp.concatenate([local, joint[3 * RANK :]], axis=0)
    for copy in range(sums.shape[0]):
        sums[copy] = both
    for y in range(CY):
        grad_a[y] = jnp.where(even, cube[1][y], cube[0][y])
        grad_b[y] = jnp.where(even, cube[0][y], cube[1][y])


def gradient_kernel(wait, block, upper_out, lower_out, planes, upper, lower, sem):
    here_a, here_b, from_a, from_b, middle, grad_a, grad_b, error = block
    wait(0, 1, 2, 3, 4)
    across = rows_across(middle, middle[2], middle[3])
    fill_planes(planes, here_a, here_b, from_a, from_b, across)
    wait(5, 6)
    even = is_even()
    side_a = jnp.concatenate([grad_a[y] for y in range(CY)], axis=1)
    side_b = jnp.concatenate([grad_b[y] for y in range(CY)], axis=1)
    grads = (jnp.where(even, side_b, side_a), jnp.where(even, side_a, side_b))
    wait(7)
    leaving = []
    for pair in range(9):
        span = pl.ds(pair * GROUP, GROUP)
        part = error[:, span]
        for x in range(CX):
            part = part + lax.dot_general(
                grads[x], window(planes, x, pair // 3, pair % 3), NT, preferred_element_type=F32
            )
        rounded = part.astype(BF16)
        upper[:, span] = rounded
        lower[:, span] = (part - rounded.astype(F32)).astype(BF16)
        for side, (held, out) in enumerate(((upper, upper_out), (lower, lower_out))):
            leaving.append(
                pltpu.make_async_copy(held.at[:, span], out.at[:, span], sem.at[2 * pair + side])
            )
            leaving[-1].start()
    for transfer in leaving:
        transfer.wait()


def fold_kernel(parts, copies):
    total = parts[0]
    for source in range(1, parts.shape[0]):
        total = total + parts[source]
    for copy in range(copies.shape[0]):
        copies[copy] = total


def project_kernel(wait, held, parts, factor_p, bias_grad, blocks, *, devices):
    upper, lower = held
    sums = parts[0]
    for source in range(1, parts.shape[0]):
        sums = sums + parts[source]
    bias_grad[...] = sums[RANK : RANK + 1] / devices
    rows = sums[:RANK]
    done = []
    for r in range(RANK):
        vector = rows[r : r + 1]
        vector = vector / jnp.sqrt(jnp.sum(vector * vector, axis=1, keepdims=True) + 1e-06)
        done.append(vector)
        rows = rows - jnp.sum(rows * vector, axis=1, keepdims=True) * vector
    basis = jnp.concatenate(done, axis=0)
    factor_p[...] = basis
    first, second, third = pieces(basis)
    stacked = jnp.concatenate([first, second, third, jnp.zeros_like(basis)], axis=0).astype(BF16)
    wait(0, 1)
    q = lax.dot_general(stacked, upper[...], NN, preferred_element_type=F32)
    q = q + lax.dot_general(stacked, lower[...], NN, preferred_element_type=F32)
    q = q[:RANK] + q[RANK : 2 * RANK] + q[2 * RANK : 3 * RANK]
    for block in range(blocks.shape[0]):
        if block < TAPS:
            blocks[block] = q[:, block * C : (block + 1) * C]
        else:
            blocks[block] = jnp.zeros((RANK, C), F32)


def residual_kernel(wait, held, out, new_error, sem):
    basis, blocks, upper, lower = held
    wait(0, 1)
    b1, b2, b3 = pieces(basis[...])
    left = jnp.concatenate([b1, b2, b3, b1, b2, b1], axis=0).astype(BF16)
    q = jnp.concatenate([blocks[tap] for tap in range(TAPS)], axis=1)
    q1, q2, q3 = pieces(q)
    right = jnp.concatenate([q1, q1, q1, q2, q2, q3], axis=0).astype(BF16)
    wait(2, 3)
    leaving = []
    for pair in range(9):
        span = pl.ds(pair * GROUP, GROUP)
        merged = upper[:, span].astype(F32) + lower[:, span].astype(F32)
        new_error[:, span] = merged - lax.dot_general(
            left, right[:, pair * GROUP : (pair + 1) * GROUP], TN, preferred_element_type=F32
        )
        leaving.append(pltpu.make_async_copy(new_error.at[:, span], out.at[:, span], sem.at[pair]))
        leaving[-1].start()
    for transfer in leaving:
        transfer.wait()


def finish_kernel(blocks, factor_q, *, devices):
    for tap in range(TAPS):
        factor_q[:, pl.ds(tap * C, C)] = blocks[tap] / devices


def backward_kernel(wait, held, out, planes):
    here_a, here_b, from_a, from_b, middle, weights = held
    wait(0, 1, 2, 3, 4)
    across = rows_across(middle, from_a[CY], from_b[CY])
    fill_planes(planes, here_a, here_b, from_a, from_b, across)
    wait(5)
    totals = [None] * CX
    for pair in range(9):
        taps = [TAPS - 1 - 3 * pair - c for c in range(3)]
        stack = jnp.concatenate([weights[tap] for tap in taps], axis=0)
        for x in range(CX):
            part = lax.dot_general(
                stack, window(planes, x, pair // 3, pair % 3), TN, preferred_element_type=F32
            )
            totals[x] = part if totals[x] is None else totals[x] + part
    for x in range(CX):
        out[:, x] = totals[x].astype(BF16).reshape(C, CY, CZ)


def pack_kernel(here_a, here_b, middle, to_a, to_b):
    even = is_even()
    for y in range(CY):
        to_a[y] = here_a[y]
        to_b[y] = here_b[y]
    to_a[CY] = jnp.where(even, middle[1], middle[0])
    to_b[CY] = jnp.where(even, middle[0], middle[1])


def swap_cores(edge):
    return lax.ppermute(edge, "sy", [(0, 1), (1, 0)])


def pairs_of(count):
    pairs_a = [(i, i ^ 1) for i in range(count) if i ^ 1 < count]
    pairs_b = [(i, j) for i in range(1, count) for j in [((i - 1) ^ 1) + 1] if j < count]
    return pairs_a, pairs_b


def exchange_x(to_a, to_b):
    pairs_a, pairs_b = pairs_of(lax.axis_size("sx"))
    return lax.ppermute(to_a, "sx", pairs_a), lax.ppermute(to_b, "sx", pairs_b)


tie = lax.optimization_barrier


def size_of(axes):
    count = 1
    for axis in axes:
        count = count * lax.axis_size(axis)
    return count


def swap(x, axes):
    return lax.all_to_all(x, axes, 0, 0, tiled=True)


def call(kernel, name, room, shapes, args, scratch=(), outs=VMEM):
    return pl.pallas_call(
        kernel,
        out_shape=shapes,
        in_specs=[VMEM] * len(args),
        out_specs=jax.tree.map(lambda _: outs, shapes),
        scratch_shapes=list(scratch),
        compiler_params=pltpu.CompilerParams(vmem_limit_bytes=room * MIB),
        name=name,
    )(*args)


def fetch_and_call(kernel, name, room, shapes, args, scratch=(), outs=VMEM, near=()):
    count = len(args)

    def body(*refs):
        close, refs = refs[: len(near)], refs[len(near) :]
        sources, rest = refs[:count], refs[count:]
        results = len(jax.tree.leaves(shapes))
        held, sem = rest[results : results + count], rest[results + count]
        copies = [
            pltpu.make_async_copy(source, target, sem.at[k])
            for k, (source, target) in enumerate(zip(sources, held))
        ]
        for copy in copies:
            copy.start()

        def wait(*which):
            for k in which:
                copies[k].wait()

        kernel(wait, held, *close, *rest[:results], *rest[results + count + 1 :])

    return pl.pallas_call(
        body,
        out_shape=shapes,
        in_specs=[VMEM] * len(near) + [HBM] * count,
        out_specs=jax.tree.map(lambda _: outs, shapes),
        scratch_shapes=[
            *(pltpu.VMEM(arg.shape, arg.dtype) for arg in args),
            pltpu.SemaphoreType.DMA((count,)),
            *scratch,
        ],
        compiler_params=pltpu.CompilerParams(vmem_limit_bytes=room * MIB),
        name=name,
    )(*near, *args)


def fold(parts, count):
    shape = jax.ShapeDtypeStruct((count,) + parts.shape[1:], F32)
    return call(fold_kernel, "fold", 2, shape, (parts,))


def f32(*shape):
    return jax.ShapeDtypeStruct(shape, F32)


def bf16(*shape):
    return jax.ShapeDtypeStruct(shape, BF16)


def shards(features, cotangent, weights, conv_bias, error_state, warm_factor):
    chips, columns = size_of(DP), size_of(BLOCK)
    devices = chips * columns
    padded = -(-TAPS // columns) * columns
    planes = pltpu.VMEM((GROUP, PX * PY * CZ), BF16)
    error = error_state[0, 0, 0]
    here_a, here_b = call(
        relayout_kernel, "relayout", 4, (bf16(CY, C, CZ), bf16(CY, C, CZ)), (features[0],)
    )
    from_a, from_b = exchange_x(here_a, here_b)
    base = call(base_kernel, "base", 4, f32(RANK, C), (warm_factor, error))
    from_a, from_b, base = tie((from_a, from_b, base))
    edge = call(edge_kernel, "edge", 2, bf16(PX, C, CZ), (here_a, here_b, from_a, from_b))
    block = (here_a, here_b, from_a, from_b, swap_cores(edge))
    act, grad_a, grad_b, edges, sums = call(
        forward_kernel,
        "forward",
        12,
        (
            bf16(C, CX, CY, CZ),
            bf16(CY, C, CZ),
            bf16(CY, C, CZ),
            bf16(CX, C, CZ),
            f32(chips, 2 * RANK, C),
        ),
        (*block, cotangent[0], weights, warm_factor, conv_bias[None], base),
        [planes],
    )
    parts = swap(sums, DP)
    upper, lower = fetch_and_call(
        gradient_kernel,
        "gradient",
        60,
        (bf16(C, K), bf16(C, K)),
        (*block, grad_a, grad_b, error),
        [planes, pltpu.VMEM((C, K), BF16), pltpu.VMEM((C, K), BF16), pltpu.SemaphoreType.DMA((18,))],
        HBM,
    )
    parts, upper, lower, edges = tie((parts, upper, lower, edges))
    parts = swap(fold(parts, columns), BLOCK)
    parts, middle = tie((parts, swap_cores(edges)))
    factor_p, bias_grad, blocks = fetch_and_call(
        functools.partial(project_kernel, devices=devices),
        "project",
        53,
        (f32(RANK, C), f32(1, C), f32(padded, RANK, C)),
        (upper, lower),
        near=(parts,),
    )
    new_error = fetch_and_call(
        residual_kernel,
        "residual",
        60,
        f32(C, K),
        (factor_p, blocks, upper, lower),
        [pltpu.VMEM((C, K), F32), pltpu.SemaphoreType.DMA((9,))],
        HBM,
    )
    width = padded // columns * RANK
    mine = swap(blocks, BLOCK)
    mine, new_error, middle, near_a, near_b = tie((mine, new_error, middle, grad_a, grad_b))
    mine = swap(fold(mine.reshape(columns, width, C), chips), DP)
    to_a, to_b = call(
        pack_kernel,
        "pack",
        4,
        (bf16(CY + 1, C, CZ), bf16(CY + 1, C, CZ)),
        (near_a, near_b, middle),
    )
    g_from_a, g_from_b = exchange_x(to_a, to_b)
    blocks = swap(fold(mine, columns), BLOCK).reshape(padded, RANK, C)
    input_grad = fetch_and_call(
        backward_kernel,
        "backward",
        40,
        bf16(C, CX, CY, CZ),
        (near_a, near_b, g_from_a, g_from_b, middle, weights),
        [planes],
    )
    factor_q = call(
        functools.partial(finish_kernel, devices=devices), "finish", 2, f32(RANK, K), (blocks,)
    )
    return (
        act[None],
        input_grad[None],
        bias_grad[0],
        factor_p,
        factor_q,
        new_error[None, None, None],
    )


def solution(mesh):
    torus = Mesh(mesh.devices.reshape(4, 8, mesh.shape["sx"], mesh.shape["sy"]), ALL_AXES)
    split = P(DP, None, "sx", "sy", None)
    state = P(DP, "sx", "sy", None, None)
    return jax.shard_map(
        shards,
        mesh=torus,
        in_specs=(split, split, P(), P(), state, P()),
        out_specs=(split, split, P(), P(), P(), state),
        check_vma=False,
    )
```

```python
import functools

import jax
import jax.numpy as jnp
from jax import lax
from jax.experimental import pallas as pl
from jax.experimental.pallas import tpu as pltpu
from jax.sharding import Mesh
from jax.sharding import PartitionSpec as P

DP = ("dp_0", "dp_1")
BLOCK = ("sx", "sy")
ALL_AXES = ("dp_0", "dp_1", "sx", "sy")
C = 128
CX = 2
CY = 4
CZ = 128
PX = CX + 2
PY = CY + 2
TAPS = 27
K = TAPS * C
RANK = 4
GROUP = 3 * C
EXTRA = 4 * RANK
F32 = jnp.float32
BF16 = jnp.bfloat16
NT = (((1,), (1,)), ((), ()))
NN = (((1,), (0,)), ((), ()))
TN = (((0,), (0,)), ((), ()))
HIGHEST = lax.Precision.HIGHEST
VMEM = pl.BlockSpec(memory_space=pltpu.VMEM)
HBM = pl.BlockSpec(memory_space=pltpu.HBM)
MIB = 1024 * 1024


def is_even():
    return lax.rem(lax.axis_index("sx"), 2) == 0


def rows_of(planes, here_a, here_b, from_a, from_b, across):
    even = is_even()
    ascending = (from_b, here_b, here_a, from_a)
    descending = (from_a, here_a, here_b, from_b)
    for xp in range(PX):
        for y in range(CY):
            yield xp, y + 1, jnp.where(even, ascending[xp][y], descending[xp][y])
    first = lax.axis_index("sy") == 0
    for xp in range(PX):
        edge = across(xp)
        nothing = jnp.zeros_like(edge)
        yield xp, 0, jnp.where(first, nothing, edge)
        yield xp, PY - 1, jnp.where(first, edge, nothing)


def fill_planes(planes, *sources):
    lane = lax.broadcasted_iota(jnp.int32, (C, CZ), 1)
    zero = jnp.zeros((C, CZ), F32)
    for xp, yp, block in rows_of(planes, *sources):
        where = pl.ds((xp * PY + yp) * CZ, CZ)
        wide = block.astype(F32)
        before = jnp.where(lane == 0, zero, pltpu.roll(wide, 1, 1))
        after = jnp.where(lane == CZ - 1, zero, pltpu.roll(wide, CZ - 1, 1))
        planes[pl.ds(0, C), where] = before.astype(BF16)
        planes[pl.ds(C, C), where] = block
        planes[pl.ds(2 * C, C), where] = after.astype(BF16)


def window(planes, x, a, b):
    return planes[:, pl.ds(((x + a) * PY + b) * CZ, CY * CZ)]


def pieces(x):
    first = x.astype(BF16).astype(F32)
    rest = x - first
    second = rest.astype(BF16).astype(F32)
    third = (rest - second).astype(BF16).astype(F32)
    return first, second, third


def relayout_kernel(cube, here_a, here_b):
    even = is_even()
    flat = [cube[:, x].reshape(C, CY * CZ) for x in range(CX)]
    for y in range(CY):
        low, high = (flat[x][:, y * CZ : (y + 1) * CZ] for x in range(CX))
        here_a[y] = jnp.where(even, high, low)
        here_b[y] = jnp.where(even, low, high)


def edge_kernel(here_a, here_b, from_a, from_b, edge):
    first = lax.axis_index("sy") == 0
    even = is_even()
    border = [jnp.where(first, plane[CY - 1], plane[0]) for plane in (here_a, here_b, from_a, from_b)]
    edge[0] = jnp.where(even, border[1], border[0])
    edge[1] = jnp.where(even, border[0], border[1])
    edge[2] = border[2]
    edge[3] = border[3]


def base_kernel(warm, error, base):
    base[...] = lax.dot_general(
        warm[...], error[...], NT, precision=HIGHEST, preferred_element_type=F32
    )


def rows_across(middle, corner_a, corner_b):
    even = is_even()

    def across(xp):
        if 0 < xp < PX - 1:
            return middle[xp - 1]
        return jnp.where(even == (xp > 0), corner_a, corner_b)

    return across


def forward_kernel(
    here_a, here_b, from_a, from_b, middle, upstream,
    weights, warm, bias, base,
    act, grad_a, grad_b, sums, planes,
):
    across = rows_across(middle, middle[2], middle[3])
    fill_planes(planes, here_a, here_b, from_a, from_b, across)
    even = is_even()
    offset = jnp.transpose(jnp.broadcast_to(bias[...], (C, C)))[:, :1]
    rows = warm[...]
    terms = jnp.concatenate([*pieces(rows), jnp.zeros_like(rows)], axis=0).astype(BF16)
    totals = [None] * CX
    for pair in range(9):
        stack = jnp.concatenate([weights[3 * pair + c] for c in range(3)], axis=1)
        span = slice(pair * GROUP, (pair + 1) * GROUP)
        stack = jnp.concatenate([stack, terms[:, span]], axis=0)
        for x in range(CX):
            part = lax.dot_general(
                stack, window(planes, x, pair // 3, pair % 3), NN, preferred_element_type=F32
            )
            totals[x] = part if totals[x] is None else totals[x] + part
    joint = jnp.zeros((EXTRA, C), F32)
    cube = []
    for x in range(CX):
        total = totals[x]
        pre = total[:C] + offset
        sigma = jax.nn.sigmoid(pre)
        slope = sigma * (1.0 + pre * (1.0 - sigma))
        act[:, x] = (pre * sigma).astype(BF16).reshape(C, CY, CZ)
        above = upstream[:, x].reshape(C, CY * CZ).astype(F32)
        gradient = (above * slope).astype(BF16)
        grads = [gradient[:, y * CZ : (y + 1) * CZ] for y in range(CY)]
        cube.append(grads)
        field = total[C : C + RANK] + total[C + RANK : C + 2 * RANK]
        field = field + total[C + 2 * RANK : C + 3 * RANK]
        stacked = jnp.concatenate([*pieces(field), jnp.ones_like(field)], axis=0)
        joint = joint + lax.dot_general(
            stacked.astype(BF16), gradient, NT, preferred_element_type=F32
        )
    local = joint[:RANK] + joint[RANK : 2 * RANK] + joint[2 * RANK : 3 * RANK] + base[...]
    both = jnp.concatenate([local, joint[3 * RANK :]], axis=0)
    for copy in range(sums.shape[0]):
        sums[copy] = both
    for y in range(CY):
        grad_a[y] = jnp.where(even, cube[1][y], cube[0][y])
        grad_b[y] = jnp.where(even, cube[0][y], cube[1][y])


def gradient_kernel(wait, block, upper_out, lower_out, planes, upper, lower, sem):
    here_a, here_b, from_a, from_b, middle, grad_a, grad_b, error = block
    wait(0, 1, 2, 3, 4)
    across = rows_across(middle, middle[2], middle[3])
    fill_planes(planes, here_a, here_b, from_a, from_b, across)
    wait(5, 6)
    even = is_even()
    side_a = jnp.concatenate([grad_a[y] for y in range(CY)], axis=1)
    side_b = jnp.concatenate([grad_b[y] for y in range(CY)], axis=1)
    grads = (jnp.where(even, side_b, side_a), jnp.where(even, side_a, side_b))
    wait(7)
    leaving = []
    for pair in range(9):
        span = pl.ds(pair * GROUP, GROUP)
        part = error[:, span]
        for x in range(CX):
            part = part + lax.dot_general(
                grads[x], window(planes, x, pair // 3, pair % 3), NT, preferred_element_type=F32
            )
        rounded = part.astype(BF16)
        upper[:, span] = rounded
        lower[:, span] = (part - rounded.astype(F32)).astype(BF16)
        for side, (held, out) in enumerate(((upper, upper_out), (lower, lower_out))):
            leaving.append(
                pltpu.make_async_copy(held.at[:, span], out.at[:, span], sem.at[2 * pair + side])
            )
            leaving[-1].start()
    for transfer in leaving:
        transfer.wait()


def fold_kernel(parts, copies):
    total = parts[0]
    for source in range(1, parts.shape[0]):
        total = total + parts[source]
    for copy in range(copies.shape[0]):
        copies[copy] = total


def project_kernel(wait, held, parts, factor_p, bias_grad, blocks, *, devices):
    upper, lower = held
    sums = parts[0]
    for source in range(1, parts.shape[0]):
        sums = sums + parts[source]
    bias_grad[...] = sums[RANK : RANK + 1] / devices
    rows = sums[:RANK]
    done = []
    for r in range(RANK):
        vector = rows[r : r + 1]
        vector = vector / jnp.sqrt(jnp.sum(vector * vector, axis=1, keepdims=True) + 1e-06)
        done.append(vector)
        rows = rows - jnp.sum(rows * vector, axis=1, keepdims=True) * vector
    basis = jnp.concatenate(done, axis=0)
    factor_p[...] = basis
    first, second, third = pieces(basis)
    stacked = jnp.concatenate([first, second, third, jnp.zeros_like(basis)], axis=0).astype(BF16)
    wait(0, 1)
    q = lax.dot_general(stacked, upper[...], NN, preferred_element_type=F32)
    q = q + lax.dot_general(stacked, lower[...], NN, preferred_element_type=F32)
    q = q[:RANK] + q[RANK : 2 * RANK] + q[2 * RANK : 3 * RANK]
    for block in range(blocks.shape[0]):
        if block < TAPS:
            blocks[block] = q[:, block * C : (block + 1) * C]
        else:
            blocks[block] = jnp.zeros((RANK, C), F32)


def residual_kernel(wait, held, out, new_error, sem):
    basis, blocks, upper, lower = held
    wait(0, 1)
    b1, b2, b3 = pieces(basis[...])
    left = jnp.concatenate([b1, b2, b3, b1, b2, b1], axis=0).astype(BF16)
    q = jnp.concatenate([blocks[tap] for tap in range(TAPS)], axis=1)
    q1, q2, q3 = pieces(q)
    right = jnp.concatenate([q1, q1, q1, q2, q2, q3], axis=0).astype(BF16)
    wait(2, 3)
    leaving = []
    for pair in range(9):
        span = pl.ds(pair * GROUP, GROUP)
        merged = upper[:, span].astype(F32) + lower[:, span].astype(F32)
        new_error[:, span] = merged - lax.dot_general(
            left, right[:, pair * GROUP : (pair + 1) * GROUP], TN, preferred_element_type=F32
        )
        leaving.append(pltpu.make_async_copy(new_error.at[:, span], out.at[:, span], sem.at[pair]))
        leaving[-1].start()
    for transfer in leaving:
        transfer.wait()


def finish_kernel(blocks, factor_q, *, devices):
    for tap in range(TAPS):
        factor_q[:, pl.ds(tap * C, C)] = blocks[tap] / devices


def backward_kernel(wait, held, out, planes):
    here_a, here_b, from_a, from_b, middle, weights = held
    wait(0, 1, 2, 3, 4)
    across = rows_across(middle, middle[2], middle[3])
    fill_planes(planes, here_a, here_b, from_a, from_b, across)
    wait(5)
    totals = [None] * CX
    for pair in range(9):
        taps = [TAPS - 1 - 3 * pair - c for c in range(3)]
        stack = jnp.concatenate([weights[tap] for tap in taps], axis=0)
        for x in range(CX):
            part = lax.dot_general(
                stack, window(planes, x, pair // 3, pair % 3), TN, preferred_element_type=F32
            )
            totals[x] = part if totals[x] is None else totals[x] + part
    for x in range(CX):
        out[:, x] = totals[x].astype(BF16).reshape(C, CY, CZ)


def swap_cores(edge):
    return lax.ppermute(edge, "sy", [(0, 1), (1, 0)])


def pairs_of(count):
    pairs_a = [(i, i ^ 1) for i in range(count) if i ^ 1 < count]
    pairs_b = [(i, j) for i in range(1, count) for j in [((i - 1) ^ 1) + 1] if j < count]
    return pairs_a, pairs_b


def exchange_x(to_a, to_b):
    pairs_a, pairs_b = pairs_of(lax.axis_size("sx"))
    return lax.ppermute(to_a, "sx", pairs_a), lax.ppermute(to_b, "sx", pairs_b)


tie = lax.optimization_barrier


def size_of(axes):
    count = 1
    for axis in axes:
        count = count * lax.axis_size(axis)
    return count


def swap(x, axes):
    return lax.all_to_all(x, axes, 0, 0, tiled=True)


def call(kernel, name, room, shapes, args, scratch=(), outs=VMEM):
    return pl.pallas_call(
        kernel,
        out_shape=shapes,
        in_specs=[VMEM] * len(args),
        out_specs=jax.tree.map(lambda _: outs, shapes),
        scratch_shapes=list(scratch),
        compiler_params=pltpu.CompilerParams(vmem_limit_bytes=room * MIB),
        name=name,
    )(*args)


def fetch_and_call(kernel, name, room, shapes, args, scratch=(), outs=VMEM, near=()):
    count = len(args)

    def body(*refs):
        close, refs = refs[: len(near)], refs[len(near) :]
        sources, rest = refs[:count], refs[count:]
        results = len(jax.tree.leaves(shapes))
        held, sem = rest[results : results + count], rest[results + count]
        copies = [
            pltpu.make_async_copy(source, target, sem.at[k])
            for k, (source, target) in enumerate(zip(sources, held))
        ]
        for copy in copies:
            copy.start()

        def wait(*which):
            for k in which:
                copies[k].wait()

        kernel(wait, held, *close, *rest[:results], *rest[results + count + 1 :])

    return pl.pallas_call(
        body,
        out_shape=shapes,
        in_specs=[VMEM] * len(near) + [HBM] * count,
        out_specs=jax.tree.map(lambda _: outs, shapes),
        scratch_shapes=[
            *(pltpu.VMEM(arg.shape, arg.dtype) for arg in args),
            pltpu.SemaphoreType.DMA((count,)),
            *scratch,
        ],
        compiler_params=pltpu.CompilerParams(vmem_limit_bytes=room * MIB),
        name=name,
    )(*near, *args)


def fold(parts, count):
    shape = jax.ShapeDtypeStruct((count,) + parts.shape[1:], F32)
    return call(fold_kernel, "fold", 2, shape, (parts,))


def f32(*shape):
    return jax.ShapeDtypeStruct(shape, F32)


def bf16(*shape):
    return jax.ShapeDtypeStruct(shape, BF16)


def shards(features, cotangent, weights, conv_bias, error_state, warm_factor):
    chips, columns = size_of(DP), size_of(BLOCK)
    devices = chips * columns
    padded = -(-TAPS // columns) * columns
    planes = pltpu.VMEM((GROUP, PX * PY * CZ), BF16)
    error = error_state[0, 0, 0]
    here_a, here_b = call(
        relayout_kernel, "relayout", 4, (bf16(CY, C, CZ), bf16(CY, C, CZ)), (features[0],)
    )
    from_a, from_b = exchange_x(here_a, here_b)
    base = call(base_kernel, "base", 4, f32(RANK, C), (warm_factor, error))
    from_a, from_b, base = tie((from_a, from_b, base))
    edge = call(edge_kernel, "edge", 2, bf16(PX, C, CZ), (here_a, here_b, from_a, from_b))
    block = (here_a, here_b, from_a, from_b, swap_cores(edge))
    act, grad_a, grad_b, sums = call(
        forward_kernel,
        "forward",
        12,
        (
            bf16(C, CX, CY, CZ),
            bf16(CY, C, CZ),
            bf16(CY, C, CZ),
            f32(chips, 2 * RANK, C),
        ),
        (*block, cotangent[0], weights, warm_factor, conv_bias[None], base),
        [planes],
    )
    parts = swap(sums, DP)
    upper, lower = fetch_and_call(
        gradient_kernel,
        "gradient",
        60,
        (bf16(C, K), bf16(C, K)),
        (*block, grad_a, grad_b, error),
        [planes, pltpu.VMEM((C, K), BF16), pltpu.VMEM((C, K), BF16), pltpu.SemaphoreType.DMA((18,))],
        HBM,
    )
    parts, upper, lower, near_a, near_b = tie((parts, upper, lower, grad_a, grad_b))
    parts = swap(fold(parts, columns), BLOCK)
    g_from_a, g_from_b = exchange_x(near_a, near_b)
    factor_p, bias_grad, blocks = fetch_and_call(
        functools.partial(project_kernel, devices=devices),
        "project",
        53,
        (f32(RANK, C), f32(1, C), f32(padded, RANK, C)),
        (upper, lower),
        near=(parts,),
    )
    new_error = fetch_and_call(
        residual_kernel,
        "residual",
        60,
        f32(C, K),
        (factor_p, blocks, upper, lower),
        [pltpu.VMEM((C, K), F32), pltpu.SemaphoreType.DMA((9,))],
        HBM,
    )
    width = padded // columns * RANK
    mine = swap(blocks, BLOCK)
    mine, new_error, g_from_a, g_from_b = tie((mine, new_error, g_from_a, g_from_b))
    mine = swap(fold(mine.reshape(columns, width, C), chips), DP)
    planes_here = (near_a, near_b, g_from_a, g_from_b)
    middle = swap_cores(call(edge_kernel, "edge", 2, bf16(PX, C, CZ), planes_here))
    mine, middle = tie((mine, middle))
    blocks = swap(fold(mine, columns), BLOCK).reshape(padded, RANK, C)
    input_grad = fetch_and_call(
        backward_kernel,
        "backward",
        40,
        bf16(C, CX, CY, CZ),
        (*planes_here, middle, weights),
        [planes],
    )
    factor_q = call(
        functools.partial(finish_kernel, devices=devices), "finish", 2, f32(RANK, K), (blocks,)
    )
    return (
        act[None],
        input_grad[None],
        bias_grad[0],
        factor_p,
        factor_q,
        new_error[None, None, None],
    )


def solution(mesh):
    torus = Mesh(mesh.devices.reshape(4, 8, mesh.shape["sx"], mesh.shape["sy"]), ALL_AXES)
    split = P(DP, None, "sx", "sy", None)
    state = P(DP, "sx", "sy", None, None)
    return jax.shard_map(
        shards,
        mesh=torus,
        in_specs=(split, split, P(), P(), state, P()),
        out_specs=(split, split, P(), P(), P(), state),
        check_vma=False,
    )
```

```python
import functools

import jax
import jax.numpy as jnp
from jax import lax
from jax.experimental import pallas as pl
from jax.experimental.pallas import tpu as pltpu
from jax.sharding import Mesh
from jax.sharding import PartitionSpec as P

DP = ("dp_0", "dp_1")
BLOCK = ("sx", "sy")
ALL_AXES = ("dp_0", "dp_1", "sx", "sy")
C = 128
CX = 2
CY = 4
CZ = 128
PX = CX + 2
PY = CY + 2
TAPS = 27
K = TAPS * C
RANK = 4
GROUP = 3 * C
EXTRA = 4 * RANK
F32 = jnp.float32
BF16 = jnp.bfloat16
NT = (((1,), (1,)), ((), ()))
NN = (((1,), (0,)), ((), ()))
TN = (((0,), (0,)), ((), ()))
HIGHEST = lax.Precision.HIGHEST
VMEM = pl.BlockSpec(memory_space=pltpu.VMEM)
HBM = pl.BlockSpec(memory_space=pltpu.HBM)
MIB = 1024 * 1024


def is_even():
    return lax.rem(lax.axis_index("sx"), 2) == 0


def rows_of(planes, here_a, here_b, from_a, from_b, across):
    even = is_even()
    ascending = (from_b, here_b, here_a, from_a)
    descending = (from_a, here_a, here_b, from_b)
    for xp in range(PX):
        for y in range(CY):
            yield xp, y + 1, jnp.where(even, ascending[xp][y], descending[xp][y])
    first = lax.axis_index("sy") == 0
    for xp in range(PX):
        edge = across(xp)
        nothing = jnp.zeros_like(edge)
        yield xp, 0, jnp.where(first, nothing, edge)
        yield xp, PY - 1, jnp.where(first, edge, nothing)


def fill_planes(planes, *sources):
    lane = lax.broadcasted_iota(jnp.int32, (C, CZ), 1)
    zero = jnp.zeros((C, CZ), F32)
    for xp, yp, block in rows_of(planes, *sources):
        where = pl.ds((xp * PY + yp) * CZ, CZ)
        wide = block.astype(F32)
        before = jnp.where(lane == 0, zero, pltpu.roll(wide, 1, 1))
        after = jnp.where(lane == CZ - 1, zero, pltpu.roll(wide, CZ - 1, 1))
        planes[pl.ds(0, C), where] = before.astype(BF16)
        planes[pl.ds(C, C), where] = block
        planes[pl.ds(2 * C, C), where] = after.astype(BF16)


def window(planes, x, a, b):
    return planes[:, pl.ds(((x + a) * PY + b) * CZ, CY * CZ)]


def pieces(x):
    first = x.astype(BF16).astype(F32)
    rest = x - first
    second = rest.astype(BF16).astype(F32)
    third = (rest - second).astype(BF16).astype(F32)
    return first, second, third


def relayout_kernel(cube, here_a, here_b):
    even = is_even()
    flat = [cube[:, x].reshape(C, CY * CZ) for x in range(CX)]
    for y in range(CY):
        low, high = (flat[x][:, y * CZ : (y + 1) * CZ] for x in range(CX))
        here_a[y] = jnp.where(even, high, low)
        here_b[y] = jnp.where(even, low, high)


def edge_kernel(here_a, here_b, from_a, from_b, edge):
    first = lax.axis_index("sy") == 0
    even = is_even()
    border = [jnp.where(first, plane[CY - 1], plane[0]) for plane in (here_a, here_b, from_a, from_b)]
    edge[0] = jnp.where(even, border[1], border[0])
    edge[1] = jnp.where(even, border[0], border[1])
    edge[2] = border[2]
    edge[3] = border[3]


def base_kernel(warm, error, base):
    base[...] = lax.dot_general(
        warm[...], error[...], NT, precision=HIGHEST, preferred_element_type=F32
    )


def rows_across(middle, corner_a, corner_b):
    even = is_even()

    def across(xp):
        if 0 < xp < PX - 1:
            return middle[xp - 1]
        return jnp.where(even == (xp > 0), corner_a, corner_b)

    return across


def forward_kernel(
    here_a, here_b, from_a, from_b, middle, upstream,
    weights, warm, bias, base,
    act, grad, edges, sums, planes,
):
    across = rows_across(middle, middle[2], middle[3])
    fill_planes(planes, here_a, here_b, from_a, from_b, across)
    first_core = lax.axis_index("sy") == 0
    even = is_even()
    offset = jnp.transpose(jnp.broadcast_to(bias[...], (C, C)))[:, :1]
    rows = warm[...]
    terms = jnp.concatenate([*pieces(rows), jnp.zeros_like(rows)], axis=0).astype(BF16)
    totals = [None] * CX
    for pair in range(9):
        stack = jnp.concatenate([weights[3 * pair + c] for c in range(3)], axis=1)
        span = slice(pair * GROUP, (pair + 1) * GROUP)
        stack = jnp.concatenate([stack, terms[:, span]], axis=0)
        for x in range(CX):
            part = lax.dot_general(
                stack, window(planes, x, pair // 3, pair % 3), NN, preferred_element_type=F32
            )
            totals[x] = part if totals[x] is None else totals[x] + part
    joint = jnp.zeros((EXTRA, C), F32)
    cube = []
    for x in range(CX):
        total = totals[x]
        pre = total[:C] + offset
        sigma = jax.nn.sigmoid(pre)
        slope = sigma * (1.0 + pre * (1.0 - sigma))
        act[:, x] = (pre * sigma).astype(BF16).reshape(C, CY, CZ)
        above = upstream[:, x].reshape(C, CY * CZ).astype(F32)
        gradient = (above * slope).astype(BF16)
        grads = [gradient[:, y * CZ : (y + 1) * CZ] for y in range(CY)]
        cube.append(grads)
        edges[x] = jnp.where(first_core, grads[CY - 1], grads[0])
        field = total[C : C + RANK] + total[C + RANK : C + 2 * RANK]
        field = field + total[C + 2 * RANK : C + 3 * RANK]
        stacked = jnp.concatenate([*pieces(field), jnp.ones_like(field)], axis=0)
        joint = joint + lax.dot_general(
            stacked.astype(BF16), gradient, NT, preferred_element_type=F32
        )
    local = joint[:RANK] + joint[RANK : 2 * RANK] + joint[2 * RANK : 3 * RANK] + base[...]
    both = jnp.concatenate([local, joint[3 * RANK :]], axis=0)
    for copy in range(sums.shape[0]):
        sums[copy] = both
    for y in range(CY):
        grad[0, y] = jnp.where(even, cube[1][y], cube[0][y])
        grad[1, y] = jnp.where(even, cube[0][y], cube[1][y])


def gradient_kernel(wait, block, upper_out, lower_out, planes, upper, lower, sem):
    here_a, here_b, from_a, from_b, middle, grad, error = block
    wait(0, 1, 2, 3, 4)
    across = rows_across(middle, middle[2], middle[3])
    fill_planes(planes, here_a, here_b, from_a, from_b, across)
    wait(5)
    even = is_even()
    side_a = jnp.concatenate([grad[0, y] for y in range(CY)], axis=1)
    side_b = jnp.concatenate([grad[1, y] for y in range(CY)], axis=1)
    grads = (jnp.where(even, side_b, side_a), jnp.where(even, side_a, side_b))
    wait(6)
    leaving = []
    for pair in range(9):
        span = pl.ds(pair * GROUP, GROUP)
        part = error[:, span]
        for x in range(CX):
            part = part + lax.dot_general(
                grads[x], window(planes, x, pair // 3, pair % 3), NT, preferred_element_type=F32
            )
        rounded = part.astype(BF16)
        upper[:, span] = rounded
        lower[:, span] = (part - rounded.astype(F32)).astype(BF16)
        for side, (held, out) in enumerate(((upper, upper_out), (lower, lower_out))):
            leaving.append(
                pltpu.make_async_copy(held.at[:, span], out.at[:, span], sem.at[2 * pair + side])
            )
            leaving[-1].start()
    for transfer in leaving:
        transfer.wait()


def fold_kernel(parts, copies):
    total = parts[0]
    for source in range(1, parts.shape[0]):
        total = total + parts[source]
    for copy in range(copies.shape[0]):
        copies[copy] = total


def project_kernel(wait, held, parts, factor_p, bias_grad, blocks, *, devices):
    upper, lower = held
    sums = parts[0]
    for source in range(1, parts.shape[0]):
        sums = sums + parts[source]
    bias_grad[...] = sums[RANK : RANK + 1] / devices
    rows = sums[:RANK]
    done = []
    for r in range(RANK):
        vector = rows[r : r + 1]
        vector = vector / jnp.sqrt(jnp.sum(vector * vector, axis=1, keepdims=True) + 1e-06)
        done.append(vector)
        rows = rows - jnp.sum(rows * vector, axis=1, keepdims=True) * vector
    basis = jnp.concatenate(done, axis=0)
    factor_p[...] = basis
    first, second, third = pieces(basis)
    stacked = jnp.concatenate([first, second, third, jnp.zeros_like(basis)], axis=0).astype(BF16)
    wait(0, 1)
    q = lax.dot_general(stacked, upper[...], NN, preferred_element_type=F32)
    q = q + lax.dot_general(stacked, lower[...], NN, preferred_element_type=F32)
    q = q[:RANK] + q[RANK : 2 * RANK] + q[2 * RANK : 3 * RANK]
    for block in range(blocks.shape[0]):
        if block < TAPS:
            blocks[block] = q[:, block * C : (block + 1) * C]
        else:
            blocks[block] = jnp.zeros((RANK, C), F32)


def residual_kernel(wait, held, out, new_error, sem):
    basis, blocks, upper, lower = held
    wait(0, 1)
    b1, b2, b3 = pieces(basis[...])
    left = jnp.concatenate([b1, b2, b3, b1, b2, b1], axis=0).astype(BF16)
    q = jnp.concatenate([blocks[tap] for tap in range(TAPS)], axis=1)
    q1, q2, q3 = pieces(q)
    right = jnp.concatenate([q1, q1, q1, q2, q2, q3], axis=0).astype(BF16)
    wait(2, 3)
    leaving = []
    for pair in range(9):
        span = pl.ds(pair * GROUP, GROUP)
        merged = upper[:, span].astype(F32) + lower[:, span].astype(F32)
        new_error[:, span] = merged - lax.dot_general(
            left, right[:, pair * GROUP : (pair + 1) * GROUP], TN, preferred_element_type=F32
        )
        leaving.append(pltpu.make_async_copy(new_error.at[:, span], out.at[:, span], sem.at[pair]))
        leaving[-1].start()
    for transfer in leaving:
        transfer.wait()


def finish_kernel(blocks, factor_q, *, devices):
    for tap in range(TAPS):
        factor_q[:, pl.ds(tap * C, C)] = blocks[tap] / devices


def backward_kernel(wait, held, out, planes):
    grad, from_a, from_b, middle, weights = held
    wait(0, 1, 2, 3)
    across = rows_across(middle, from_a[CY], from_b[CY])
    fill_planes(planes, grad.at[0], grad.at[1], from_a, from_b, across)
    wait(4)
    totals = [None] * CX
    for pair in range(9):
        taps = [TAPS - 1 - 3 * pair - c for c in range(3)]
        stack = jnp.concatenate([weights[tap] for tap in taps], axis=0)
        for x in range(CX):
            part = lax.dot_general(
                stack, window(planes, x, pair // 3, pair % 3), TN, preferred_element_type=F32
            )
            totals[x] = part if totals[x] is None else totals[x] + part
    for x in range(CX):
        out[:, x] = totals[x].astype(BF16).reshape(C, CY, CZ)


def pack_kernel(grad, middle, to_a, to_b):
    even = is_even()
    for y in range(CY):
        to_a[y] = grad[0, y]
        to_b[y] = grad[1, y]
    to_a[CY] = jnp.where(even, middle[1], middle[0])
    to_b[CY] = jnp.where(even, middle[0], middle[1])


def swap_cores(edge):
    return lax.ppermute(edge, "sy", [(0, 1), (1, 0)])


def pairs_of(count):
    pairs_a = [(i, i ^ 1) for i in range(count) if i ^ 1 < count]
    pairs_b = [(i, j) for i in range(1, count) for j in [((i - 1) ^ 1) + 1] if j < count]
    return pairs_a, pairs_b


def exchange_x(to_a, to_b):
    pairs_a, pairs_b = pairs_of(lax.axis_size("sx"))
    return lax.ppermute(to_a, "sx", pairs_a), lax.ppermute(to_b, "sx", pairs_b)


tie = lax.optimization_barrier


def size_of(axes):
    count = 1
    for axis in axes:
        count = count * lax.axis_size(axis)
    return count


def swap(x, axes):
    return lax.all_to_all(x, axes, 0, 0, tiled=True)


def call(kernel, name, room, shapes, args, scratch=(), outs=VMEM):
    return pl.pallas_call(
        kernel,
        out_shape=shapes,
        in_specs=[VMEM] * len(args),
        out_specs=jax.tree.map(lambda _: outs, shapes),
        scratch_shapes=list(scratch),
        compiler_params=pltpu.CompilerParams(vmem_limit_bytes=room * MIB),
        name=name,
    )(*args)


def fetch_and_call(kernel, name, room, shapes, args, scratch=(), outs=VMEM, near=()):
    count = len(args)

    def body(*refs):
        close, refs = refs[: len(near)], refs[len(near) :]
        sources, rest = refs[:count], refs[count:]
        results = len(jax.tree.leaves(shapes))
        held, sem = rest[results : results + count], rest[results + count]
        copies = [
            pltpu.make_async_copy(source, target, sem.at[k])
            for k, (source, target) in enumerate(zip(sources, held))
        ]
        for copy in copies:
            copy.start()

        def wait(*which):
            for k in which:
                copies[k].wait()

        kernel(wait, held, *close, *rest[:results], *rest[results + count + 1 :])

    return pl.pallas_call(
        body,
        out_shape=shapes,
        in_specs=[VMEM] * len(near) + [HBM] * count,
        out_specs=jax.tree.map(lambda _: outs, shapes),
        scratch_shapes=[
            *(pltpu.VMEM(arg.shape, arg.dtype) for arg in args),
            pltpu.SemaphoreType.DMA((count,)),
            *scratch,
        ],
        compiler_params=pltpu.CompilerParams(vmem_limit_bytes=room * MIB),
        name=name,
    )(*near, *args)


def fold(parts, count):
    shape = jax.ShapeDtypeStruct((count,) + parts.shape[1:], F32)
    return call(fold_kernel, "fold", 2, shape, (parts,))


def f32(*shape):
    return jax.ShapeDtypeStruct(shape, F32)


def bf16(*shape):
    return jax.ShapeDtypeStruct(shape, BF16)


def shards(features, cotangent, weights, conv_bias, error_state, warm_factor):
    chips, columns = size_of(DP), size_of(BLOCK)
    devices = chips * columns
    padded = -(-TAPS // columns) * columns
    planes = pltpu.VMEM((GROUP, PX * PY * CZ), BF16)
    error = error_state[0, 0, 0]
    here_a, here_b = call(
        relayout_kernel, "relayout", 4, (bf16(CY, C, CZ), bf16(CY, C, CZ)), (features[0],)
    )
    from_a, from_b = exchange_x(here_a, here_b)
    base = call(base_kernel, "base", 4, f32(RANK, C), (warm_factor, error))
    from_a, from_b, base = tie((from_a, from_b, base))
    edge = call(edge_kernel, "edge", 2, bf16(PX, C, CZ), (here_a, here_b, from_a, from_b))
    block = (here_a, here_b, from_a, from_b, swap_cores(edge))
    act, grad, edges, sums = call(
        forward_kernel,
        "forward",
        12,
        (
            bf16(C, CX, CY, CZ),
            bf16(CX, CY, C, CZ),
            bf16(CX, C, CZ),
            f32(chips, 2 * RANK, C),
        ),
        (*block, cotangent[0], weights, warm_factor, conv_bias[None], base),
        [planes],
    )
    parts = swap(sums, DP)
    upper, lower = fetch_and_call(
        gradient_kernel,
        "gradient",
        60,
        (bf16(C, K), bf16(C, K)),
        (*block, grad, error),
        [planes, pltpu.VMEM((C, K), BF16), pltpu.VMEM((C, K), BF16), pltpu.SemaphoreType.DMA((18,))],
        HBM,
    )
    parts, upper, lower, edges = tie((parts, upper, lower, edges))
    parts = swap(fold(parts, columns), BLOCK)
    parts, middle = tie((parts, swap_cores(edges)))
    factor_p, bias_grad, blocks = fetch_and_call(
        functools.partial(project_kernel, devices=devices),
        "project",
        53,
        (f32(RANK, C), f32(1, C), f32(padded, RANK, C)),
        (upper, lower),
        near=(parts,),
    )
    new_error = fetch_and_call(
        residual_kernel,
        "residual",
        60,
        f32(C, K),
        (factor_p, blocks, upper, lower),
        [pltpu.VMEM((C, K), F32), pltpu.SemaphoreType.DMA((9,))],
        HBM,
    )
    width = padded // columns * RANK
    mine = swap(blocks, BLOCK)
    mine, new_error, middle, grad = tie((mine, new_error, middle, grad))
    mine = swap(fold(mine.reshape(columns, width, C), chips), DP)
    to_a, to_b = call(
        pack_kernel,
        "pack",
        4,
        (bf16(CY + 1, C, CZ), bf16(CY + 1, C, CZ)),
        (grad, middle),
    )
    g_from_a, g_from_b = exchange_x(to_a, to_b)
    blocks = swap(fold(mine, columns), BLOCK).reshape(padded, RANK, C)
    input_grad = fetch_and_call(
        backward_kernel,
        "backward",
        40,
        bf16(C, CX, CY, CZ),
        (grad, g_from_a, g_from_b, middle, weights),
        [planes],
    )
    factor_q = call(
        functools.partial(finish_kernel, devices=devices), "finish", 2, f32(RANK, K), (blocks,)
    )
    return (
        act[None],
        input_grad[None],
        bias_grad[0],
        factor_p,
        factor_q,
        new_error[None, None, None],
    )


def solution(mesh):
    torus = Mesh(mesh.devices.reshape(4, 8, mesh.shape["sx"], mesh.shape["sy"]), ALL_AXES)
    split = P(DP, None, "sx", "sy", None)
    state = P(DP, "sx", "sy", None, None)
    return jax.shard_map(
        shards,
        mesh=torus,
        in_specs=(split, split, P(), P(), state, P()),
        out_specs=(split, split, P(), P(), P(), state),
        check_vma=False,
    )
```

```python
import functools

import jax
import jax.numpy as jnp
from jax import lax
from jax.experimental import pallas as pl
from jax.experimental.pallas import tpu as pltpu
from jax.sharding import Mesh
from jax.sharding import PartitionSpec as P

DP = ("dp_0", "dp_1")
BLOCK = ("sx", "sy")
ALL_AXES = ("dp_0", "dp_1", "sx", "sy")
C = 128
CX = 2
CY = 4
CZ = 128
PX = CX + 2
PY = CY + 2
TAPS = 27
K = TAPS * C
RANK = 4
GROUP = 3 * C
EXTRA = 4 * RANK
F32 = jnp.float32
BF16 = jnp.bfloat16
NT = (((1,), (1,)), ((), ()))
NN = (((1,), (0,)), ((), ()))
TN = (((0,), (0,)), ((), ()))
HIGHEST = lax.Precision.HIGHEST
VMEM = pl.BlockSpec(memory_space=pltpu.VMEM)
HBM = pl.BlockSpec(memory_space=pltpu.HBM)
MIB = 1024 * 1024


def is_even():
    return lax.rem(lax.axis_index("sx"), 2) == 0


def rows_of(planes, here_a, here_b, from_a, from_b, across):
    even = is_even()
    ascending = (from_b, here_b, here_a, from_a)
    descending = (from_a, here_a, here_b, from_b)
    for xp in range(PX):
        for y in range(CY):
            yield xp, y + 1, jnp.where(even, ascending[xp][y], descending[xp][y])
    first = lax.axis_index("sy") == 0
    for xp in range(PX):
        edge = across(xp)
        nothing = jnp.zeros_like(edge)
        yield xp, 0, jnp.where(first, nothing, edge)
        yield xp, PY - 1, jnp.where(first, edge, nothing)


def fill_planes(planes, *sources):
    lane = lax.broadcasted_iota(jnp.int32, (C, CZ), 1)
    zero = jnp.zeros((C, CZ), F32)
    for xp, yp, block in rows_of(planes, *sources):
        where = pl.ds((xp * PY + yp) * CZ, CZ)
        wide = block.astype(F32)
        before = jnp.where(lane == 0, zero, pltpu.roll(wide, 1, 1))
        after = jnp.where(lane == CZ - 1, zero, pltpu.roll(wide, CZ - 1, 1))
        planes[pl.ds(0, C), where] = before.astype(BF16)
        planes[pl.ds(C, C), where] = block
        planes[pl.ds(2 * C, C), where] = after.astype(BF16)


def window(planes, x, a, b):
    return planes[:, pl.ds(((x + a) * PY + b) * CZ, CY * CZ)]


def pieces(x):
    first = x.astype(BF16).astype(F32)
    rest = x - first
    second = rest.astype(BF16).astype(F32)
    third = (rest - second).astype(BF16).astype(F32)
    return first, second, third


def relayout_kernel(cube, here_a, here_b):
    even = is_even()
    flat = [cube[:, x].reshape(C, CY * CZ) for x in range(CX)]
    for y in range(CY):
        low, high = (flat[x][:, y * CZ : (y + 1) * CZ] for x in range(CX))
        here_a[y] = jnp.where(even, high, low)
        here_b[y] = jnp.where(even, low, high)


def edge_kernel(here_a, here_b, from_a, from_b, edge):
    first = lax.axis_index("sy") == 0
    even = is_even()
    border = [jnp.where(first, plane[CY - 1], plane[0]) for plane in (here_a, here_b, from_a, from_b)]
    edge[0] = jnp.where(even, border[1], border[0])
    edge[1] = jnp.where(even, border[0], border[1])
    edge[2] = border[2]
    edge[3] = border[3]


def base_kernel(warm, error, base):
    base[...] = lax.dot_general(
        warm[...], error[...], NT, precision=HIGHEST, preferred_element_type=F32
    )


def rows_across(middle, corner_a, corner_b):
    even = is_even()

    def across(xp):
        if 0 < xp < PX - 1:
            return middle[xp - 1]
        return jnp.where(even == (xp > 0), corner_a, corner_b)

    return across


def forward_kernel(
    here_a, here_b, from_a, from_b, middle, upstream,
    weights, warm, bias, base,
    act, grad, edges, sums, planes,
):
    across = rows_across(middle, middle[2], middle[3])
    fill_planes(planes, here_a, here_b, from_a, from_b, across)
    first_core = lax.axis_index("sy") == 0
    even = is_even()
    offset = jnp.transpose(jnp.broadcast_to(bias[...], (C, C)))[:, :1]
    rows = warm[...]
    terms = jnp.concatenate([*pieces(rows), jnp.zeros_like(rows)], axis=0).astype(BF16)
    totals = [None] * CX
    for pair in range(9):
        stack = jnp.concatenate([weights[3 * pair + c] for c in range(3)], axis=1)
        span = slice(pair * GROUP, (pair + 1) * GROUP)
        stack = jnp.concatenate([stack, terms[:, span]], axis=0)
        for x in range(CX):
            part = lax.dot_general(
                stack, window(planes, x, pair // 3, pair % 3), NN, preferred_element_type=F32
            )
            totals[x] = part if totals[x] is None else totals[x] + part
    joint = jnp.zeros((EXTRA, C), F32)
    cube = []
    for x in range(CX):
        total = totals[x]
        pre = total[:C] + offset
        sigma = jax.nn.sigmoid(pre)
        slope = sigma * (1.0 + pre * (1.0 - sigma))
        act[:, x] = (pre * sigma).astype(BF16).reshape(C, CY, CZ)
        above = upstream[:, x].reshape(C, CY * CZ).astype(F32)
        gradient = (above * slope).astype(BF16)
        grads = [gradient[:, y * CZ : (y + 1) * CZ] for y in range(CY)]
        cube.append(grads)
        edges[x] = jnp.where(first_core, grads[CY - 1], grads[0])
        field = total[C : C + RANK] + total[C + RANK : C + 2 * RANK]
        field = field + total[C + 2 * RANK : C + 3 * RANK]
        stacked = jnp.concatenate([*pieces(field), jnp.ones_like(field)], axis=0)
        joint = joint + lax.dot_general(
            stacked.astype(BF16), gradient, NT, preferred_element_type=F32
        )
    local = joint[:RANK] + joint[RANK : 2 * RANK] + joint[2 * RANK : 3 * RANK] + base[...]
    both = jnp.concatenate([local, joint[3 * RANK :]], axis=0)
    for copy in range(sums.shape[0]):
        sums[copy] = both
    for y in range(CY):
        grad[0, y] = jnp.where(even, cube[1][y], cube[0][y])
        grad[1, y] = jnp.where(even, cube[0][y], cube[1][y])


def gradient_kernel(wait, block, upper_out, lower_out, planes, upper, lower, sem):
    here_a, here_b, from_a, from_b, middle, grad, error = block
    wait(0, 1, 2, 3, 4)
    across = rows_across(middle, middle[2], middle[3])
    fill_planes(planes, here_a, here_b, from_a, from_b, across)
    wait(5)
    even = is_even()
    side_a = jnp.concatenate([grad[0, y] for y in range(CY)], axis=1)
    side_b = jnp.concatenate([grad[1, y] for y in range(CY)], axis=1)
    grads = (jnp.where(even, side_b, side_a), jnp.where(even, side_a, side_b))
    wait(6)
    leaving = []
    for pair in range(9):
        span = pl.ds(pair * GROUP, GROUP)
        part = error[:, span]
        for x in range(CX):
            part = part + lax.dot_general(
                grads[x], window(planes, x, pair // 3, pair % 3), NT, preferred_element_type=F32
            )
        rounded = part.astype(BF16)
        upper[:, span] = rounded
        lower[:, span] = (part - rounded.astype(F32)).astype(BF16)
        for side, (held, out) in enumerate(((upper, upper_out), (lower, lower_out))):
            leaving.append(
                pltpu.make_async_copy(held.at[:, span], out.at[:, span], sem.at[2 * pair + side])
            )
            leaving[-1].start()
    for transfer in leaving:
        transfer.wait()


def fold_kernel(parts, copies):
    total = parts[0]
    for source in range(1, parts.shape[0]):
        total = total + parts[source]
    for copy in range(copies.shape[0]):
        copies[copy] = total


def project_kernel(wait, held, parts, factor_p, bias_grad, blocks, *, devices):
    upper, lower = held
    sums = parts[0]
    for source in range(1, parts.shape[0]):
        sums = sums + parts[source]
    bias_grad[...] = sums[RANK : RANK + 1] / devices
    rows = sums[:RANK]
    done = []
    for r in range(RANK):
        vector = rows[r : r + 1]
        vector = vector / jnp.sqrt(jnp.sum(vector * vector, axis=1, keepdims=True) + 1e-06)
        done.append(vector)
        rows = rows - jnp.sum(rows * vector, axis=1, keepdims=True) * vector
    basis = jnp.concatenate(done, axis=0)
    factor_p[...] = basis
    first, second, third = pieces(basis)
    stacked = jnp.concatenate([first, second, third, jnp.zeros_like(basis)], axis=0).astype(BF16)
    wait(0, 1)
    q = lax.dot_general(stacked, upper[...], NN, preferred_element_type=F32)
    q = q + lax.dot_general(stacked, lower[...], NN, preferred_element_type=F32)
    q = q[:RANK] + q[RANK : 2 * RANK] + q[2 * RANK : 3 * RANK]
    for block in range(blocks.shape[0]):
        if block < TAPS:
            blocks[block] = q[:, block * C : (block + 1) * C]
        else:
            blocks[block] = jnp.zeros((RANK, C), F32)


def residual_kernel(wait, held, out, new_error, sem):
    basis, blocks, upper, lower = held
    wait(0, 1)
    b1, b2, _ = pieces(basis[...])
    left = jnp.concatenate([b1, b1, b2, jnp.zeros_like(b1)], axis=0).astype(BF16)
    q1, q2, _ = pieces(jnp.concatenate([blocks[tap] for tap in range(TAPS)], axis=1))
    right = jnp.concatenate([q1, q2, q1, jnp.zeros_like(q1)], axis=0).astype(BF16)
    wait(2, 3)
    leaving = []
    for pair in range(9):
        span = pl.ds(pair * GROUP, GROUP)
        merged = upper[:, span].astype(F32) + lower[:, span].astype(F32)
        new_error[:, span] = merged - lax.dot_general(
            left, right[:, pair * GROUP : (pair + 1) * GROUP], TN, preferred_element_type=F32
        )
        leaving.append(pltpu.make_async_copy(new_error.at[:, span], out.at[:, span], sem.at[pair]))
        leaving[-1].start()
    for transfer in leaving:
        transfer.wait()


def finish_kernel(blocks, factor_q, *, devices):
    for tap in range(TAPS):
        factor_q[:, pl.ds(tap * C, C)] = blocks[tap] / devices


def backward_kernel(wait, held, out, planes):
    grad, from_a, from_b, middle, weights = held
    wait(0, 1, 2, 3)
    across = rows_across(middle, from_a[CY], from_b[CY])
    fill_planes(planes, grad.at[0], grad.at[1], from_a, from_b, across)
    wait(4)
    totals = [None] * CX
    for pair in range(9):
        taps = [TAPS - 1 - 3 * pair - c for c in range(3)]
        stack = jnp.concatenate([weights[tap] for tap in taps], axis=0)
        for x in range(CX):
            part = lax.dot_general(
                stack, window(planes, x, pair // 3, pair % 3), TN, preferred_element_type=F32
            )
            totals[x] = part if totals[x] is None else totals[x] + part
    for x in range(CX):
        out[:, x] = totals[x].astype(BF16).reshape(C, CY, CZ)


def pack_kernel(grad, middle, to_a, to_b):
    even = is_even()
    for y in range(CY):
        to_a[y] = grad[0, y]
        to_b[y] = grad[1, y]
    to_a[CY] = jnp.where(even, middle[1], middle[0])
    to_b[CY] = jnp.where(even, middle[0], middle[1])


def swap_cores(edge):
    return lax.ppermute(edge, "sy", [(0, 1), (1, 0)])


def pairs_of(count):
    pairs_a = [(i, i ^ 1) for i in range(count) if i ^ 1 < count]
    pairs_b = [(i, j) for i in range(1, count) for j in [((i - 1) ^ 1) + 1] if j < count]
    return pairs_a, pairs_b


def exchange_x(to_a, to_b):
    pairs_a, pairs_b = pairs_of(lax.axis_size("sx"))
    return lax.ppermute(to_a, "sx", pairs_a), lax.ppermute(to_b, "sx", pairs_b)


tie = lax.optimization_barrier


def size_of(axes):
    count = 1
    for axis in axes:
        count = count * lax.axis_size(axis)
    return count


def swap(x, axes):
    return lax.all_to_all(x, axes, 0, 0, tiled=True)


def call(kernel, name, room, shapes, args, scratch=(), outs=VMEM):
    return pl.pallas_call(
        kernel,
        out_shape=shapes,
        in_specs=[VMEM] * len(args),
        out_specs=jax.tree.map(lambda _: outs, shapes),
        scratch_shapes=list(scratch),
        compiler_params=pltpu.CompilerParams(vmem_limit_bytes=room * MIB),
        name=name,
    )(*args)


def fetch_and_call(kernel, name, room, shapes, args, scratch=(), outs=VMEM, near=()):
    count = len(args)

    def body(*refs):
        close, refs = refs[: len(near)], refs[len(near) :]
        sources, rest = refs[:count], refs[count:]
        results = len(jax.tree.leaves(shapes))
        held, sem = rest[results : results + count], rest[results + count]
        copies = [
            pltpu.make_async_copy(source, target, sem.at[k])
            for k, (source, target) in enumerate(zip(sources, held))
        ]
        for copy in copies:
            copy.start()

        def wait(*which):
            for k in which:
                copies[k].wait()

        kernel(wait, held, *close, *rest[:results], *rest[results + count + 1 :])

    return pl.pallas_call(
        body,
        out_shape=shapes,
        in_specs=[VMEM] * len(near) + [HBM] * count,
        out_specs=jax.tree.map(lambda _: outs, shapes),
        scratch_shapes=[
            *(pltpu.VMEM(arg.shape, arg.dtype) for arg in args),
            pltpu.SemaphoreType.DMA((count,)),
            *scratch,
        ],
        compiler_params=pltpu.CompilerParams(vmem_limit_bytes=room * MIB),
        name=name,
    )(*near, *args)


def fold(parts, count):
    shape = jax.ShapeDtypeStruct((count,) + parts.shape[1:], F32)
    return call(fold_kernel, "fold", 2, shape, (parts,))


def f32(*shape):
    return jax.ShapeDtypeStruct(shape, F32)


def bf16(*shape):
    return jax.ShapeDtypeStruct(shape, BF16)


def shards(features, cotangent, weights, conv_bias, error_state, warm_factor):
    chips, columns = size_of(DP), size_of(BLOCK)
    devices = chips * columns
    padded = -(-TAPS // columns) * columns
    planes = pltpu.VMEM((GROUP, PX * PY * CZ), BF16)
    error = error_state[0, 0, 0]
    here_a, here_b = call(
        relayout_kernel, "relayout", 4, (bf16(CY, C, CZ), bf16(CY, C, CZ)), (features[0],)
    )
    from_a, from_b = exchange_x(here_a, here_b)
    base = call(base_kernel, "base", 4, f32(RANK, C), (warm_factor, error))
    from_a, from_b, base = tie((from_a, from_b, base))
    edge = call(edge_kernel, "edge", 2, bf16(PX, C, CZ), (here_a, here_b, from_a, from_b))
    block = (here_a, here_b, from_a, from_b, swap_cores(edge))
    act, grad, edges, sums = call(
        forward_kernel,
        "forward",
        12,
        (
            bf16(C, CX, CY, CZ),
            bf16(CX, CY, C, CZ),
            bf16(CX, C, CZ),
            f32(chips, 2 * RANK, C),
        ),
        (*block, cotangent[0], weights, warm_factor, conv_bias[None], base),
        [planes],
    )
    parts = swap(sums, DP)
    upper, lower = fetch_and_call(
        gradient_kernel,
        "gradient",
        60,
        (bf16(C, K), bf16(C, K)),
        (*block, grad, error),
        [planes, pltpu.VMEM((C, K), BF16), pltpu.VMEM((C, K), BF16), pltpu.SemaphoreType.DMA((18,))],
        HBM,
    )
    parts, upper, lower, edges = tie((parts, upper, lower, edges))
    parts = swap(fold(parts, columns), BLOCK)
    parts, middle = tie((parts, swap_cores(edges)))
    factor_p, bias_grad, blocks = fetch_and_call(
        functools.partial(project_kernel, devices=devices),
        "project",
        53,
        (f32(RANK, C), f32(1, C), f32(padded, RANK, C)),
        (upper, lower),
        near=(parts,),
    )
    new_error = fetch_and_call(
        residual_kernel,
        "residual",
        60,
        f32(C, K),
        (factor_p, blocks, upper, lower),
        [pltpu.VMEM((C, K), F32), pltpu.SemaphoreType.DMA((9,))],
        HBM,
    )
    width = padded // columns * RANK
    mine = swap(blocks, BLOCK)
    mine, new_error, middle, grad = tie((mine, new_error, middle, grad))
    mine = swap(fold(mine.reshape(columns, width, C), chips), DP)
    to_a, to_b = call(
        pack_kernel,
        "pack",
        4,
        (bf16(CY + 1, C, CZ), bf16(CY + 1, C, CZ)),
        (grad, middle),
    )
    g_from_a, g_from_b = exchange_x(to_a, to_b)
    blocks = swap(fold(mine, columns), BLOCK).reshape(padded, RANK, C)
    input_grad = fetch_and_call(
        backward_kernel,
        "backward",
        40,
        bf16(C, CX, CY, CZ),
        (grad, g_from_a, g_from_b, middle, weights),
        [planes],
    )
    factor_q = call(
        functools.partial(finish_kernel, devices=devices), "finish", 2, f32(RANK, K), (blocks,)
    )
    return (
        act[None],
        input_grad[None],
        bias_grad[0],
        factor_p,
        factor_q,
        new_error[None, None, None],
    )


def solution(mesh):
    torus = Mesh(mesh.devices.reshape(4, 8, mesh.shape["sx"], mesh.shape["sy"]), ALL_AXES)
    split = P(DP, None, "sx", "sy", None)
    state = P(DP, "sx", "sy", None, None)
    return jax.shard_map(
        shards,
        mesh=torus,
        in_specs=(split, split, P(), P(), state, P()),
        out_specs=(split, split, P(), P(), P(), state),
        check_vma=False,
    )
```
